32 devices in a mesh: groups: 2 (over y), wide: 16 (over z, x, core).
Axes of the slice: x: 2, y: 2, z: 4, core: 2. Of those that a mesh axis runs over, the one named last changes fastest.
Arguments:
- rows: bfloat16 [16384, 768], P(('groups', 'wide')), parts along dimension 0, may hold values from -6 to 6
- cell: int32 [16384], P(('groups', 'wide')), parts along dimension 0, may hold values from 0 to 511, as said below
- cell_place: int32 [1024], P('groups'), parts along dimension 0, may hold values from 0 to 511, as said below
- coarse: bfloat16 [1024, 768], P(('groups', 'wide')), parts along dimension 0, may hold values from -6 to 6
- fine: bfloat16 [1024, 64, 768], P(('groups', 'wide')), parts along dimension 0, may hold values from -6 to 6
- reseed: int32 [1024, 64], P(('groups', 'wide')), parts along dimension 0, may hold values from 0 to 511
Outputs:
- row_error: float32 [16384], P(('groups', 'wide')), parts along dimension 0
- coarse_new: float32 [1024, 768], P(('groups', 'wide')), parts along dimension 0
- fine_new: float32 [1024, 64, 768], P(('groups', 'wide')), parts along dimension 0
The draws below stay inside these ranges and needn't reach their ends.
There are 2 independent parts, one for each index of `groups`. The reference program is written for one: setup_inputs(seed, part) draws one part's arguments, and reference() takes and returns one part's arrays. A program takes and returns all parts, laid end to end along the dimension named above; each array names one. Nothing has to cross between parts.
Inputs may be any that keep to these rules, and one draw needn't show every extreme that they name: `cell`: the rows of one index of wide name at most 64 rows whose cells are owned by one index of wide, and exactly 64 for some owner in every draw. `cell_place`: each place appears once.
All inputs are finite; a program needn't handle non-finite values.
Results may differ from the reference program's by a relative error of at most 0.0045.
Values may be sent and summed in bfloat16 or wider, within the bound.
No kernel may reach another device: no remote copies, remote signals or barrier semaphores. Data moves between devices by JAX's collectives and lax.ppermute only.
A program may use at most 64 MiB of HBM per device.

```python
import jax
import jax.numpy as jnp
from jax import lax

D = 768
CELLS_DEV = 32
FINE = 64
ROWS_DEV = 512
CELLS = 512
ROWS = 8192
CAP = 64
TEMP = 16


def shared_place(key):
    return jax.random.permutation(key, CELLS).astype(jnp.int32)


def draw_cell_place(key, part):
    return shared_place(key)


def draw_cell(key, part):
    place = shared_place(key)
    inverse = jnp.argsort(place).astype(jnp.int32)
    key = jax.random.fold_in(key, 7)
    sources = ROWS // ROWS_DEV
    pool = sources * CAP
    labels = (jnp.arange(pool, dtype=jnp.int32) // CAP).astype(jnp.int32)
    keys = jax.random.split(key, sources)

    def single_source(sampling_key):
        hot_random_key, ordering_key, shuffling_key, slot_random_key = jax.random.split(sampling_key, 4)
        hotter = jax.random.randint(hot_random_key, (), 0, max(1, sources // 8))
        priority = jax.random.permutation(ordering_key, pool).astype(jnp.int32) - pool * (labels == hotter).astype(jnp.int32)
        chosen = labels[jnp.argsort(priority)[:ROWS_DEV]]
        chosen = jax.random.permutation(shuffling_key, chosen)
        slots = jax.random.randint(slot_random_key, (ROWS_DEV,), 0, CELLS_DEV)
        return inverse[chosen * CELLS_DEV + slots]
    return jax.vmap(single_source)(keys).reshape(ROWS).astype(jnp.int32)


def plant(values, stream_key, smallest, top_value):
    spot = [jax.random.randint(jax.random.fold_in(stream_key, axis), (), 0, length) for axis, length in enumerate(values.shape)]
    longest = values.shape.index(max(values.shape))
    next_to = spot[:longest] + [(spot[longest] + 1) % values.shape[longest]] + spot[longest + 1:]
    return values.at[tuple(spot)].set(smallest).at[tuple(next_to)].set(top_value)


def block_scale(rng, shape, cuts, low, largest):
    factor_of = 1.0
    for dim, parts in cuts:
        steps = jax.random.uniform(jax.random.fold_in(jax.random.fold_in(rng, 6), dim), (parts,), jnp.float32, low / len(cuts), largest / len(cuts))
        factor_of = factor_of * jnp.repeat(jnp.exp(steps), shape[dim] // parts).reshape((-1,) + (1,) * (len(shape) - 1 - dim))
    return factor_of


def gaussian(key, dims, spread, limit, pieces=(), held_as=jnp.bfloat16):
    entries = spread * jax.random.normal(key, dims, jnp.float32)
    if pieces:
        entries = entries * block_scale(key, dims, pieces, -0.22, 0.18)
    return jnp.clip(entries, -limit, limit).astype(held_as)


def setup_inputs(seed: int = 0, part: int = 0) -> dict:
    streams_of = jax.random.split(jax.random.key(seed), 7)
    part_keys = jax.random.split(jax.random.fold_in(streams_of[6], part), 7)
    rows = gaussian(part_keys[0], (ROWS, D), 1.0, 6.0, ((0, 16),))
    cell = draw_cell(jax.random.fold_in(jax.random.fold_in(streams_of[6], part), 71), part)
    cell_place = draw_cell_place(jax.random.fold_in(jax.random.fold_in(streams_of[6], part), 71), part)
    coarse = gaussian(part_keys[3], (CELLS, D), 1.0, 6.0, ((0, 16),))
    fine = gaussian(part_keys[4], (CELLS, FINE, D), 1.0, 6.0, ((0, 16),))
    reseed = plant(jax.random.randint(part_keys[5], (CELLS, FINE), 0, ROWS_DEV), jax.random.fold_in(part_keys[5], 1), 0, ROWS_DEV - 1).astype(jnp.int32)
    return {"rows": rows, "cell": cell, "cell_place": cell_place, "coarse": coarse, "fine": fine, "reseed": reseed}


def reference(rows, cell, cell_place, coarse, fine, reseed):
    place = cell_place[cell]
    resid = (rows.astype(jnp.float32) - coarse[place].astype(jnp.float32)).astype(jnp.bfloat16)
    blocks = ROWS // ROWS_DEV

    def step(carry, index):
        fsum, fcount, csum, ccount = carry
        start = index * ROWS_DEV
        partial_residual = lax.dynamic_slice_in_dim(resid, start, ROWS_DEV, 0).astype(jnp.float32)
        part_p = lax.dynamic_slice_in_dim(place, start, ROWS_DEV, 0)
        centres = fine[part_p].astype(jnp.float32)
        inner_product = jnp.einsum("bd,bfd->bf", partial_residual, centres)
        fine_squared_norm = jnp.sum(centres * centres, axis=-1)
        residual_squared_norm = jnp.sum(partial_residual * partial_residual, axis=-1)
        squared_distance = residual_squared_norm[:, None] - 2.0 * inner_product + fine_squared_norm
        logit = -squared_distance / TEMP
        peak = jnp.max(logit, axis=1)
        expo = jnp.exp(logit - peak[:, None])
        total = jnp.sum(expo, axis=1)
        weight = (expo / total[:, None]).astype(jnp.bfloat16).astype(jnp.float32)
        error = -TEMP * (peak + jnp.log(total))
        fsum = fsum.at[part_p].add(weight[:, :, None] * partial_residual[:, None, :])
        fcount = fcount.at[part_p].add(weight)
        csum = csum.at[part_p].add(partial_residual)
        ccount = ccount.at[part_p].add(jnp.ones((ROWS_DEV,), jnp.float32))
        return (fsum, fcount, csum, ccount), error

    init = (jnp.zeros((CELLS, FINE, D), jnp.float32), jnp.zeros((CELLS, FINE), jnp.float32),
            jnp.zeros((CELLS, D), jnp.float32), jnp.zeros((CELLS,), jnp.float32))
    (fsum, fcount, csum, ccount), errors = lax.scan(step, init, jnp.arange(blocks, dtype=jnp.int32))
    row_error = errors.reshape(ROWS)

    def owner_block(owner):
        first = owner * CELLS_DEV
        block_sum = lax.dynamic_slice_in_dim(fsum, first, CELLS_DEV, 0)
        block_count = lax.dynamic_slice_in_dim(fcount, first, CELLS_DEV, 0)
        block_seed = lax.dynamic_slice_in_dim(reseed, first, CELLS_DEV, 0)
        block_coarse = lax.dynamic_slice_in_dim(coarse, first, CELLS_DEV, 0).astype(jnp.float32)
        local_rows = lax.dynamic_slice_in_dim(rows, owner * ROWS_DEV, ROWS_DEV, 0)
        seedres = local_rows[block_seed].astype(jnp.float32) - block_coarse[:, None, :]
        return (block_sum + seedres) / (block_count[:, :, None] + 1.0)

    owners = ROWS // ROWS_DEV
    fine_new = lax.map(owner_block, jnp.arange(owners, dtype=jnp.int32)).reshape(CELLS, FINE, D)
    coarse_new = coarse.astype(jnp.float32) + csum / (ccount[:, None] + 1.0)
    return row_error, coarse_new, fine_new
```

```python
import functools

import jax
import jax.numpy as jnp
from jax import lax
from jax.experimental import pallas as pl
from jax.experimental.pallas import tpu as pltpu
from jax.sharding import PartitionSpec as P

TEMP = 16
LANES = 128
META = 16
VMEM_LIMIT = 48 * 1024 * 1024
BF = jnp.bfloat16
F32 = jnp.float32


def iota(shape, dim):
    return lax.broadcasted_iota(jnp.int32, shape, dim)


def hot(index, size, dtype=BF):
    return (iota((size, index.shape[1]), 0) == index).astype(F32).astype(dtype)


def dot(a, b, dims=((1,), (0,))):
    return lax.dot_general(a, b, (dims, ((), ())), preferred_element_type=F32)


def split3(x):
    high = x.astype(BF)
    rest = x - high.astype(F32)
    mid = rest.astype(BF)
    return high, mid, (rest - mid.astype(F32)).astype(BF)


def pack_kernel(peers, capacity, cells_dev, cell_ref, place_ref, rows_ref, send_ref, route_ref):
    rows_dev, width = rows_ref.shape
    cells = place_ref.shape[1]
    chunks = width // LANES
    block = chunks * capacity + META
    cell = cell_ref[...]
    place = place_ref[...]
    table_row = iota((16, cells), 0)
    table = jnp.where(
        table_row == 0, place // cells_dev, jnp.where(table_row == 1, place % cells_dev, 0)
    ).astype(F32).astype(BF)
    found = jnp.zeros((16, rows_dev), F32)
    step = min(cells, 512)
    for first in range(0, cells, step):
        found += dot(table[:, first : first + step], hot(cell - first, step))
    owner = found[0:1].astype(jnp.int32)
    local = found[1:2]
    owner_hot = hot(owner, peers, F32)
    upper = (iota((rows_dev, rows_dev), 0) <= iota((rows_dev, rows_dev), 1)).astype(F32).astype(BF)
    running = dot(owner_hot.astype(BF), upper)
    rank = (jnp.sum(running * owner_hot, axis=0, keepdims=True) - 1.0).astype(jnp.int32)
    route_ref[...] = jnp.where(iota((8, rows_dev), 0) == 0, owner, rank)
    ids = dot((owner_hot * (local + 1.0)).astype(BF), hot(rank, LANES), ((1,), (1,))).astype(BF)
    slot = owner * capacity + rank
    group = max(1, 256 // capacity)
    for first in range(0, peers, group):
        packed = dot(hot(slot - first * capacity, group * capacity), rows_ref[...]).astype(BF)
        for p in range(group):
            start = (first + p) * block
            for j in range(chunks):
                send_ref[start + j * capacity : start + (j + 1) * capacity, :] = packed[
                    p * capacity : (p + 1) * capacity, j * LANES : (j + 1) * LANES
                ]
            send_ref[start + chunks * capacity : start + block, :] = jnp.broadcast_to(
                ids[first + p : first + p + 1], (META, LANES)
            )


def score_kernel(
    peers, capacity, got_ref, coarse_ref, norm_ref, fine_ref,
    error_ref, weight_ref, resid_ref, ids_ref, best_ref, square_ref,
):
    step = pl.program_id(0)
    cells_dev, width = coarse_ref.shape
    fine_n = norm_ref.shape[1]
    slots = peers * capacity
    chunks = width // LANES
    block = chunks * capacity + META
    group = max(1, 256 // capacity)
    span = group * capacity

    @pl.when(step == 0)
    def _():
        for p in range(peers):
            start = p * block + chunks * capacity
            ids_ref[:, p * capacity : (p + 1) * capacity] = (
                got_ref[start : start + META, :].astype(F32)[0:1, :capacity].astype(jnp.int32) - 1
            )
        member = hot(ids_ref[...], cells_dev)
        for first in range(0, peers, group):
            own = dot(
                member[:, first * capacity : first * capacity + span], coarse_ref[...], ((0,), (0,))
            )
            square = jnp.zeros((span, 1), F32)
            for j in range(chunks):
                lanes = slice(j * LANES, (j + 1) * LANES)
                got = jnp.concatenate(
                    [
                        got_ref[p * block + j * capacity : p * block + (j + 1) * capacity, :]
                        for p in range(first, first + group)
                    ],
                    axis=0,
                )
                resid = (got.astype(F32) - own[:, lanes]).astype(BF)
                resid_ref[first * capacity : first * capacity + span, lanes] = resid
                wide = resid.astype(F32)
                square += jnp.sum(wide * wide, axis=1, keepdims=True)
            diagonal = iota((span, span), 0) == iota((span, span), 1)
            square_ref[:, first * capacity : first * capacity + span] = jnp.sum(
                jnp.where(diagonal, square, 0.0), axis=0, keepdims=True
            )
        best_ref[...] = jnp.zeros_like(best_ref)

    cells = fine_ref.shape[0] // fine_n
    ids = ids_ref[...]
    scores = dot(fine_ref[...], resid_ref[...], ((1,), (1,)))
    best = best_ref[...]
    for c in range(cells):
        best = jnp.where(ids == step * cells + c, scores[c * fine_n : (c + 1) * fine_n], best)
    best_ref[...] = best

    @pl.when(step == pl.num_programs(0) - 1)
    def _():
        member = hot(ids, cells_dev)
        norm = sum(dot(part, member, ((0,), (0,))) for part in split3(norm_ref[...]))
        logit = (2.0 * best_ref[...] - norm) * (1.0 / TEMP)
        peak = jnp.max(logit, axis=0, keepdims=True)
        expo = jnp.exp(logit - peak)
        total = jnp.sum(expo, axis=0, keepdims=True)
        weight_ref[...] = (expo / total).astype(BF)
        error = square_ref[...] - TEMP * (peak + jnp.log(total))
        error_ref[...] = jnp.zeros_like(error_ref)
        for p in range(peers):
            error_ref[p, :, :capacity] = error[:, p * capacity : (p + 1) * capacity]


def update_kernel(
    ids_ref, weight_ref, resid_ref, coarse_ref, seed_ref, coarse_out_ref, fine_out_ref
):
    step = pl.program_id(0)
    cells_dev, width = coarse_ref.shape
    cells, fine_n, _ = fine_out_ref.shape
    ids = ids_ref[...]
    weight = weight_ref[...].astype(F32)

    @pl.when(step == 0)
    def _():
        member = hot(ids, cells_dev, F32)
        count = jnp.sum(member, axis=1, keepdims=True)
        coarse_out_ref[...] = coarse_ref[...].astype(F32) + dot(
            member.astype(BF), resid_ref[...]
        ) / (count + 1.0)

    spread = [jnp.where(ids == step * cells + c, weight, 0.0) for c in range(cells)]
    total = dot(jnp.concatenate([s.astype(BF) for s in spread], axis=0), resid_ref[...])
    own = coarse_ref[pl.ds(step * cells, cells), :].astype(F32) if cells % 8 == 0 else None
    for c in range(cells):
        count = jnp.sum(spread[c], axis=1, keepdims=True)
        if own is None:
            hit = iota((cells_dev, 1), 0) == step * cells + c
            centre = jnp.sum(
                jnp.where(hit, coarse_ref[...].astype(F32), 0.0), axis=0, keepdims=True
            )
        else:
            centre = own[c : c + 1]
        rows = slice(c * fine_n, (c + 1) * fine_n)
        seed = seed_ref[rows, :].astype(F32) - centre
        fine_out_ref[c] = (total[rows] + seed) / (count + 1.0)


def collect_kernel(peers, route_ref, error_ref, out_ref):
    owner_hot = hot(route_ref[0:1, :], peers, F32)
    rank_hot = hot(route_ref[1:2, :], LANES)
    error = error_ref[...].reshape(peers, LANES)
    picked = sum(dot(part, rank_hot) for part in split3(error))
    out_ref[...] = jnp.sum(picked * owner_hot, axis=0, keepdims=True)


def whole(shape):
    return pl.BlockSpec(shape, lambda *_: (0,) * len(shape))


def call(kernel, grid, in_specs, out_specs, out_shape, scratch=(), flops=0, moved=0):
    return pl.pallas_call(
        kernel,
        grid=grid,
        in_specs=in_specs,
        out_specs=out_specs,
        out_shape=out_shape,
        scratch_shapes=scratch,
        compiler_params=pltpu.CompilerParams(vmem_limit_bytes=VMEM_LIMIT),
        cost_estimate=pl.CostEstimate(flops=flops, bytes_accessed=moved, transcendentals=0),
    )


def shards(rows, cell, cell_place, coarse, fine, reseed):
    peers = lax.axis_size("wide")
    rows_dev, width = rows.shape
    cells_dev, fine_n, _ = fine.shape
    cells = cell_place.shape[0]
    capacity = max(16, 2 * rows_dev // peers)
    slots = peers * capacity
    block = (width // LANES) * capacity + META
    fine_all = cells_dev * fine_n

    send, route = call(
        functools.partial(pack_kernel, peers, capacity, cells_dev),
        (1,),
        [whole((1, rows_dev)), whole((1, cells)), whole((rows_dev, width))],
        [whole((peers * block, LANES)), whole((8, rows_dev))],
        [
            jax.ShapeDtypeStruct((peers * block, LANES), BF),
            jax.ShapeDtypeStruct((8, rows_dev), jnp.int32),
        ],
        flops=2 * slots * rows_dev * width,
        moved=2 * (slots + rows_dev) * width,
    )(cell.reshape(1, rows_dev), cell_place.reshape(1, cells), rows)

    got = lax.all_to_all(
        send.reshape(peers, block, LANES), "wide", split_axis=0, concat_axis=0, tiled=False
    ).reshape(peers * block, LANES)

    fine_wide = fine.astype(F32)
    norm = jnp.sum(fine_wide * fine_wide, axis=-1)
    seed = rows[reseed.reshape(fine_all)]

    cells_step = max(1, 256 // fine_n)
    steps = cells_dev // cells_step
    tile = cells_step * fine_n
    error, weight, resid, ids = call(
        functools.partial(score_kernel, peers, capacity),
        (steps,),
        [
            whole((peers * block, LANES)),
            whole((cells_dev, width)),
            whole((cells_dev, fine_n)),
            pl.BlockSpec((tile, width), lambda i: (i, 0)),
        ],
        [
            whole((peers, 1, LANES)),
            whole((fine_n, slots)),
            whole((slots, width)),
            whole((1, slots)),
        ],
        [
            jax.ShapeDtypeStruct((peers, 1, LANES), F32),
            jax.ShapeDtypeStruct((fine_n, slots), BF),
            jax.ShapeDtypeStruct((slots, width), BF),
            jax.ShapeDtypeStruct((1, slots), jnp.int32),
        ],
        scratch=[pltpu.VMEM((fine_n, slots), F32), pltpu.VMEM((1, slots), F32)],
        flops=2 * slots * fine_all * width,
        moved=2 * (2 * slots + fine_all) * width,
    )(got, coarse, norm, fine.reshape(fine_all, width))

    returned = lax.all_to_all(error, "wide", split_axis=0, concat_axis=0, tiled=False)

    coarse_new, fine_new = call(
        update_kernel,
        (steps,),
        [
            whole((1, slots)),
            whole((fine_n, slots)),
            whole((slots, width)),
            whole((cells_dev, width)),
            pl.BlockSpec((tile, width), lambda i: (i, 0)),
        ],
        [
            whole((cells_dev, width)),
            pl.BlockSpec((cells_step, fine_n, width), lambda i: (i, 0, 0)),
        ],
        [
            jax.ShapeDtypeStruct((cells_dev, width), F32),
            jax.ShapeDtypeStruct((cells_dev, fine_n, width), F32),
        ],
        flops=2 * slots * fine_all * width,
        moved=2 * slots * width + 6 * fine_all * width,
    )(ids, weight, resid, coarse, seed)

    row_error = call(
        functools.partial(collect_kernel, peers),
        (1,),
        [whole((8, rows_dev)), whole((peers, 1, LANES))],
        whole((1, rows_dev)),
        jax.ShapeDtypeStruct((1, rows_dev), F32),
        moved=4 * (8 * rows_dev + peers * LANES),
    )(route, returned).reshape(rows_dev)
    return row_error, coarse_new, fine_new


def solution(mesh):
    in_specs = (
        P(("groups", "wide"), None),
        P(("groups", "wide")),
        P("groups"),
        P(("groups", "wide"), None),
        P(("groups", "wide"), None, None),
        P(("groups", "wide"), None),
    )
    out_specs = (
        P(("groups", "wide")),
        P(("groups", "wide"), None),
        P(("groups", "wide"), None, None),
    )
    return jax.shard_map(shards, mesh=mesh, in_specs=in_specs, out_specs=out_specs, check_vma=False)
```

```python
import functools

import jax
import jax.numpy as jnp
from jax import lax
from jax.experimental import pallas as pl
from jax.experimental.pallas import tpu as pltpu
from jax.sharding import PartitionSpec as P

TEMP = 16
LANES = 128
META = 16
VMEM_LIMIT = 24 * 1024 * 1024
BF = jnp.bfloat16
F32 = jnp.float32


def iota(shape, dim):
    return lax.broadcasted_iota(jnp.int32, shape, dim)


def hot(index, size, dtype=BF):
    return (iota((size, index.shape[1]), 0) == index).astype(F32).astype(dtype)


def dot(a, b, dims=((1,), (0,))):
    return lax.dot_general(a, b, (dims, ((), ())), preferred_element_type=F32)


def split3(x):
    high = x.astype(BF)
    rest = x - high.astype(F32)
    mid = rest.astype(BF)
    return high, mid, (rest - mid.astype(F32)).astype(BF)


def put_block(ref, base, rows, meta):
    count, width = rows.shape
    chunks = width // LANES
    whole_rows = count // 16 * 16
    for j in range(chunks):
        ref[base + j * whole_rows : base + (j + 1) * whole_rows, :] = rows[
            :whole_rows, j * LANES : (j + 1) * LANES
        ].astype(BF)
    base += chunks * whole_rows
    if count > whole_rows:
        for j in range(0, chunks, 2):
            pair = [
                rows[whole_rows:, i * LANES : (i + 1) * LANES] for i in (j, j + 1)
            ]
            ref[base : base + 16, :] = jnp.concatenate(pair, axis=0).astype(BF)
            base += 16
    ref[base : base + META, :] = meta


def get_block(ref, base, count, chunks):
    whole_rows = count // 16 * 16
    parts = [
        ref[base + j * whole_rows : base + (j + 1) * whole_rows, :].astype(F32)
        for j in range(chunks)
    ]
    if count > whole_rows:
        base += chunks * whole_rows
        for j in range(0, chunks, 2):
            pair = ref[base + j * 8 : base + j * 8 + 16, :].astype(F32)
            parts[j] = jnp.concatenate([parts[j], pair[:8]], axis=0)
            parts[j + 1] = jnp.concatenate([parts[j + 1], pair[8:]], axis=0)
    return parts


def get_meta(ref, base, count, chunks):
    first = base + chunks * count
    return ref[first : first + META, :].astype(F32)


def find_route(cells_dev, peers, cell_ref, place_ref, upper):
    rows_dev = cell_ref.shape[1]
    cells = place_ref.shape[1]
    cell = cell_ref[...]
    place = place_ref[...]
    table_row = iota((16, cells), 0)
    table = jnp.where(
        table_row == 0, place // cells_dev, jnp.where(table_row == 1, place % cells_dev, 0)
    ).astype(F32).astype(BF)
    found = jnp.zeros((16, rows_dev), F32)
    step = min(cells, 512)
    for first in range(0, cells, step):
        found += dot(table[:, first : first + step], hot(cell - first, step))
    owner = found[0:1].astype(jnp.int32)
    owner_hot = hot(owner, peers, F32)
    running = dot(owner_hot.astype(BF), upper)
    rank = (jnp.sum(running * owner_hot, axis=0, keepdims=True) - 1.0).astype(jnp.int32)
    return owner, found[1:2], rank, owner_hot


def prefix(rows_dev):
    return (iota((rows_dev, rows_dev), 0) <= iota((rows_dev, rows_dev), 1)).astype(F32).astype(BF)


def fetch(sources, targets, sems):
    copies = [
        pltpu.make_async_copy(source, target, sems.at[i])
        for i, (source, target) in enumerate(zip(sources, targets, strict=True))
    ]
    for copy in copies:
        copy.start()
    return copies


def pack_kernel(
    peers, capacity, cells_dev, cell_hbm, place_hbm, rows_hbm,
    send_hbm, route_ref, cell_ref, place_ref, rows_ref, send_ref, in_sems, out_sems,
):
    arrivals = fetch(
        (cell_hbm, place_hbm, rows_hbm), (cell_ref, place_ref, rows_ref), in_sems
    )
    rows_dev, width = rows_ref.shape
    block = (width // LANES) * capacity + META
    upper = prefix(rows_dev)
    arrivals[0].wait()
    arrivals[1].wait()
    owner, local, rank, owner_hot = find_route(cells_dev, peers, cell_ref, place_ref, upper)
    route_ref[...] = jnp.where(iota((8, rows_dev), 0) == 0, owner, rank)
    ids = dot((owner_hot * (local + 1.0)).astype(BF), hot(rank, LANES), ((1,), (1,))).astype(BF)
    slot = owner * capacity + rank
    group = max(1, 256 // capacity)
    arrivals[2].wait()
    departures = []
    for first in range(0, peers, group):
        packed = dot(hot(slot - first * capacity, group * capacity), rows_ref[...])
        for p in range(group):
            put_block(
                send_ref,
                (first + p) * block,
                packed[p * capacity : (p + 1) * capacity],
                jnp.broadcast_to(ids[first + p : first + p + 1], (META, LANES)),
            )
        part = pl.ds(first * block, group * block)
        departures.append(
            pltpu.make_async_copy(
                send_ref.at[part], send_hbm.at[part], out_sems.at[first // group]
            )
        )
        departures[-1].start()
    for copy in departures:
        copy.wait()


def pack_split_kernel(
    peers, capacity, cells_dev, distances, cell_hbm, place_hbm, rows_hbm, *refs
):
    far_hbms = refs[: len(distances)]
    (
        near_hbm, route_ref, cell_ref, place_ref, rows_ref, send_ref, in_sems, out_sems
    ) = refs[len(distances) :]
    arrivals = fetch(
        (cell_hbm, place_hbm, rows_hbm), (cell_ref, place_ref, rows_ref), in_sems
    )
    rows_dev, width = rows_ref.shape
    half = peers // 2
    block = (width // LANES) * capacity + META
    upper = prefix(rows_dev)
    me = lax.axis_index("wide")
    arrivals[0].wait()
    arrivals[1].wait()
    owner, local, rank, _ = find_route(cells_dev, peers, cell_ref, place_ref, upper)
    route_ref[...] = jnp.where(iota((8, rows_dev), 0) == 0, owner, rank)
    apart = owner ^ me
    order = owner & (half - 1)
    for i, r in enumerate(distances):
        order = jnp.where(apart == r, half + i, order)
    slot = order * capacity + rank
    ids = dot(
        (hot(order, peers, F32) * (local + 1.0)).astype(BF), hot(rank, LANES), ((1,), (1,))
    ).astype(BF)
    group = max(1, 256 // capacity)
    arrivals[2].wait()
    departures = []
    for first in range(0, peers, group):
        packed = dot(hot(slot - first * capacity, group * capacity), rows_ref[...])
        for p in range(group):
            i = first + p
            put_block(
                send_ref,
                i * block,
                packed[p * capacity : (p + 1) * capacity],
                jnp.broadcast_to(ids[i : i + 1], (META, LANES)),
            )
            target = near_hbm.at[pl.ds(i * block, block)] if i < half else far_hbms[i - half]
            departures.append(
                pltpu.make_async_copy(
                    send_ref.at[pl.ds(i * block, block)], target, out_sems.at[i]
                )
            )
            departures[-1].start()
    for copy in departures:
        copy.wait()


def seed_kernel(reseed_ref, rows_ref, seed_hbm, seed_ref, sems):
    rows_dev = rows_ref.shape[0]
    part = seed_ref.shape[0] // sems.shape[0]
    copies = []
    for i in range(sems.shape[0]):
        here = slice(i * part, (i + 1) * part)
        picked = hot(reseed_ref[:, here], rows_dev)
        seed_ref[here, :] = dot(picked, rows_ref[...], ((0,), (0,))).astype(BF)
        copies.append(
            pltpu.make_async_copy(seed_ref.at[here], seed_hbm.at[here], sems.at[i])
        )
        copies[-1].start()
    for copy in copies:
        copy.wait()


def score_kernel(blocks, capacity, far_of, known, coarse_ref, norm_ref, fine_ref, *refs):
    got_refs = refs[: len(blocks)]
    known_refs = refs[len(blocks) : len(blocks) + len(known)]
    error_ref, weight_ref, ids_ref, resid_hbm, resid_ref, sems = refs[len(blocks) + len(known) :]
    cells_dev, width = coarse_ref.shape
    fine_n = norm_ref.shape[1]
    chunks = width // LANES
    size = chunks * capacity + META
    group = max(1, 256 // capacity)
    tile = max(1, 512 // fine_n) * fine_n
    places = [(ref, b * size) for ref, count in zip(got_refs, blocks) for b in range(count)]
    error_ref[...] = jnp.zeros_like(error_ref)
    rows_of = list(range(len(places)))
    if far_of is not None:
        me = lax.axis_index("wide")
        rows_of = [me ^ r for r in far_of]
        half = error_ref.shape[0] // 2
        for ref, distances in zip(known_refs, known):
            for i in range(ref.shape[0]):
                row = (me & half) + i if distances is None else me ^ distances[i]
                error_ref[row] = ref[i]
    for p, (ref, base) in enumerate(places):
        ids_ref[:, p * capacity : (p + 1) * capacity] = (
            get_meta(ref, base, capacity, chunks)[0:1, :capacity].astype(jnp.int32) - 1
        )
    norms = split3(norm_ref[...])
    copies = []
    for first in range(0, len(places), group):
        some = places[first : first + group]
        span = len(some) * capacity
        here = slice(first * capacity, first * capacity + span)
        ids = ids_ref[:, here]
        member = hot(ids, cells_dev)
        own = dot(member, coarse_ref[...], ((0,), (0,)))
        square = jnp.zeros((span, LANES), F32)
        got = [get_block(ref, base, capacity, chunks) for ref, base in some]
        for j in range(chunks):
            lanes = slice(j * LANES, (j + 1) * LANES)
            part = (jnp.concatenate([g[j] for g in got], axis=0) - own[:, lanes]).astype(BF)
            resid_ref[here, lanes] = part
            wide = part.astype(F32)
            square += wide * wide
        resid = resid_ref[here, :]
        copies.append(
            pltpu.make_async_copy(resid_ref.at[here], resid_hbm.at[here], sems.at[first // group])
        )
        copies[-1].start()
        column = jnp.sum(square, axis=1, keepdims=True)
        diagonal = iota((span, span), 0) == iota((span, span), 1)
        square_row = jnp.sum(jnp.where(diagonal, column, 0.0), axis=0, keepdims=True)
        best = jnp.zeros((fine_n, span), F32)
        for start in range(0, cells_dev * fine_n, tile):
            scores = dot(fine_ref[start : start + tile, :], resid, ((1,), (1,)))
            for c in range(tile // fine_n):
                best = jnp.where(
                    ids == start // fine_n + c, scores[c * fine_n : (c + 1) * fine_n], best
                )
        norm = sum(dot(part, member, ((0,), (0,))) for part in norms)
        logit = (2.0 * best - norm) * (1.0 / TEMP)
        peak = jnp.max(logit, axis=0, keepdims=True)
        expo = jnp.exp(logit - peak)
        total = jnp.sum(expo, axis=0, keepdims=True)
        weight_ref[:, here] = (expo / total).astype(BF)
        error = square_row - TEMP * (peak + jnp.log(total))
        for p in range(len(some)):
            error_ref[rows_of[first + p], :, :capacity] = error[
                :, p * capacity : (p + 1) * capacity
            ]
    for copy in copies:
        copy.wait()


def update_kernel(sets, coarse_ref, *refs):
    ids_refs, weight_refs, resid_hbms = (refs[i * sets : (i + 1) * sets] for i in range(3))
    (
        seed_hbm, coarse_out_ref, fine_hbm, resid_ref, seed_ref, out_ref, spread_ref, share_ref,
        in_sems, seed_sems, out_sems,
    ) = refs[3 * sets :]
    cells_dev, width = coarse_ref.shape
    fine_n = weight_refs[0].shape[0]
    steps = out_sems.shape[0]
    cells = cells_dev // steps
    rows = cells * fine_n
    starts = [sum(r.shape[0] for r in resid_hbms[:i]) for i in range(sets)]
    arrivals = fetch(
        resid_hbms,
        [resid_ref.at[pl.ds(s, r.shape[0])] for s, r in zip(starts, resid_hbms)],
        in_sems,
    )
    half = seed_ref.shape[0] // 2
    parts = [pl.ds(0, half), pl.ds(half, half)]
    seeds = fetch([seed_hbm.at[p] for p in parts], [seed_ref.at[p] for p in parts], seed_sems)
    ids = jnp.concatenate([ref[...] for ref in ids_refs], axis=1)
    weight = jnp.concatenate([ref[...] for ref in weight_refs], axis=1).astype(F32)
    centre = coarse_ref[...].astype(F32)

    def spread(step):
        for c in range(cells):
            part = jnp.where(ids == step * cells + c, weight, 0.0)
            spread_ref[step % 2, c * fine_n : (c + 1) * fine_n, :] = part.astype(BF)
            first = step * rows + c * fine_n
            share_ref[first : first + fine_n, :] = jnp.broadcast_to(
                1.0 / (jnp.sum(part, axis=1, keepdims=True) + 1.0), (fine_n, LANES)
            )

    def finish(step):
        for c in range(cells):
            here = slice(step * rows + c * fine_n, step * rows + (c + 1) * fine_n)
            own = centre[step * cells + c : step * cells + c + 1]
            share = share_ref[here, :]
            for j in range(0, width, LANES):
                lanes = slice(j, j + LANES)
                seed = seed_ref[here, lanes].astype(F32) - own[:, lanes]
                out_ref[here, lanes] = (out_ref[here, lanes] + seed) * share
        part = pl.ds(step * rows, rows)
        copy = pltpu.make_async_copy(out_ref.at[part], fine_hbm.at[part], out_sems.at[step])
        copy.start()
        return copy

    spread(0)
    for copy in arrivals:
        copy.wait()
    departures = []
    for step in range(steps + 1):
        if step == 1:
            seeds[0].wait()
        if step == steps // 2 + 1:
            seeds[1].wait()
        if step < steps:
            out_ref[step * rows : (step + 1) * rows, :] = dot(spread_ref[step % 2], resid_ref[...])
        if step + 1 < steps:
            spread(step + 1)
        if step > 0:
            departures.append(finish(step - 1))
    member = hot(ids, cells_dev, F32)
    count = jnp.sum(member, axis=1, keepdims=True)
    coarse_out_ref[...] = centre + dot(member.astype(BF), resid_ref[...]) / (count + 1.0)
    for copy in departures:
        copy.wait()


def collect_kernel(peers, route_ref, error_ref, out_ref):
    owner_hot = hot(route_ref[0:1, :], peers, F32)
    rank_hot = hot(route_ref[1:2, :], LANES)
    error = error_ref[...].reshape(peers, LANES)
    picked = sum(dot(part, rank_hot) for part in split3(error))
    out_ref[...] = jnp.sum(picked * owner_hot, axis=0, keepdims=True)


def far(x):
    return pltpu.with_memory_space_constraint(x, pltpu.HBM)


def whole(shape):
    return pl.BlockSpec(shape, lambda *_: (0,) * len(shape))


HBM = pl.BlockSpec(memory_space=pltpu.HBM)
VMEM = pl.BlockSpec(memory_space=pltpu.VMEM)


def call(kernel, grid, in_specs, out_specs, out_shape, scratch=(), flops=0, moved=0):
    return pl.pallas_call(
        kernel,
        grid=grid,
        in_specs=in_specs,
        out_specs=out_specs,
        out_shape=out_shape,
        scratch_shapes=scratch,
        compiler_params=pltpu.CompilerParams(vmem_limit_bytes=VMEM_LIMIT),
        cost_estimate=pl.CostEstimate(flops=flops, bytes_accessed=moved, transcendentals=0),
    )


def shape_of(shape, dtype):
    return jax.ShapeDtypeStruct(shape, dtype)


def score(got, blocks, capacity, coarse, norm, fine, far_of=None, known=(), errors=(), peers=0):
    width = coarse.shape[1]
    fine_n = norm.shape[1]
    count = sum(blocks)
    slots = count * capacity
    return call(
        functools.partial(score_kernel, blocks, capacity, far_of, known),
        (),
        [VMEM] * (3 + len(got) + len(errors)),
        [VMEM, VMEM, VMEM, HBM],
        [
            shape_of((peers or count, 1, LANES), F32),
            shape_of((fine_n, slots), BF),
            shape_of((1, slots), jnp.int32),
            pltpu.HBM((slots, width), BF),
        ],
        scratch=[
            pltpu.VMEM((slots, width), BF),
            pltpu.SemaphoreType.DMA((count,)),
        ],
        flops=2 * slots * fine.shape[0] * width,
        moved=2 * (2 * slots + fine.shape[0]) * width,
    )(coarse, norm, fine, *got, *errors)


def update(scored, coarse, seed, cells_dev, fine_n):
    width = coarse.shape[1]
    fine_all = cells_dev * fine_n
    sets = len(scored)
    _, weights, ids, resids = zip(*scored)
    slots = sum(r.shape[0] for r in resids)
    steps = max(2, cells_dev // 4)
    coarse_new, fine_new = call(
        functools.partial(update_kernel, sets),
        (),
        [VMEM] * (1 + 2 * sets) + [HBM] * (sets + 1),
        [VMEM, HBM],
        [shape_of((cells_dev, width), F32), pltpu.HBM((fine_all, width), F32)],
        scratch=[
            pltpu.VMEM((slots, width), BF),
            pltpu.VMEM((fine_all, width), BF),
            pltpu.VMEM((fine_all, width), F32),
            pltpu.VMEM((2, fine_all // steps, slots), BF),
            pltpu.VMEM((fine_all, LANES), F32),
            pltpu.SemaphoreType.DMA((sets,)),
            pltpu.SemaphoreType.DMA((2,)),
            pltpu.SemaphoreType.DMA((steps,)),
        ],
        flops=2 * slots * fine_all * width,
        moved=2 * slots * width + 6 * fine_all * width,
    )(coarse, *ids, *weights, *[far(r) for r in resids], far(seed))
    return coarse_new, fine_new.reshape(cells_dev, fine_n, width)


def shards(rows, cell, cell_place, coarse, fine, reseed):
    peers = lax.axis_size("wide")
    rows_dev, width = rows.shape
    cells_dev, fine_n, _ = fine.shape
    cells = cell_place.shape[0]
    capacity = max(16, 2 * rows_dev // peers)
    slots = peers * capacity
    block = (width // LANES) * capacity + META
    fine_all = cells_dev * fine_n

    fine_wide = fine.astype(F32)
    norm = jnp.sum(fine_wide * fine_wide, axis=-1)
    fine_flat = fine.reshape(fine_all, width)
    seed = call(
        seed_kernel,
        (),
        [VMEM, VMEM],
        HBM,
        pltpu.HBM((fine_all, width), BF),
        scratch=[pltpu.VMEM((fine_all, width), BF), pltpu.SemaphoreType.DMA((4,))],
        flops=2 * fine_all * rows_dev * width,
        moved=2 * (fine_all + rows_dev) * width,
    )(reseed.reshape(1, fine_all), rows)
    cell = far(cell.reshape(1, rows_dev))
    cell_place = far(cell_place.reshape(1, cells))
    if capacity == 64 and peers == 16:
        half = peers // 2
        distances = [8, 12, 9, 13, 10, 14, 11, 15]
        *sends, near_send, route = call(
            functools.partial(pack_split_kernel, peers, capacity, cells_dev, distances),
            (),
            [HBM] * 3,
            [HBM] * (half + 1) + [VMEM],
            [
                *[pltpu.HBM((block, LANES), BF)] * half,
                pltpu.HBM((half * block, LANES), BF),
                shape_of((8, rows_dev), jnp.int32),
            ],
            scratch=[
                pltpu.VMEM((1, rows_dev), jnp.int32),
                pltpu.VMEM((1, cells), jnp.int32),
                pltpu.VMEM((rows_dev, width), BF),
                pltpu.VMEM((peers * block, LANES), BF),
                pltpu.SemaphoreType.DMA((3,)),
                pltpu.SemaphoreType.DMA((peers,)),
            ],
            flops=2 * slots * rows_dev * width,
            moved=2 * (slots + 2 * rows_dev) * width,
        )(cell, cell_place, far(rows))
        got = []
        window = 5
        for i, r in enumerate(distances):
            block_out = sends[i]
            if i >= window:
                block_out, got[i - window] = lax.optimization_barrier((block_out, got[i - window]))
            got.append(lax.ppermute(block_out, "wide", [(p, p ^ r) for p in range(peers)]))
        halves = [list(range(half)), list(range(half, peers))]
        got_near = lax.all_to_all(
            near_send.reshape(half, block, LANES), "wide", split_axis=0, concat_axis=0,
            tiled=False, axis_index_groups=halves,
        ).reshape(half * block, LANES)
        tables = (coarse, norm, fine_flat)
        scored = [score([got_near], [half], capacity, *tables)]
        scored.append(score(got[:4], [1] * 4, capacity, *tables))
        known = (None, distances[:4])
        errors = [x[0] for x in scored]
        scored.append(
            score(got[4:], [1] * 4, capacity, *tables, distances[4:], known, errors, peers)
        )
    else:
        send, route = call(
            functools.partial(pack_kernel, peers, capacity, cells_dev),
            (),
            [HBM] * 3,
            [HBM, VMEM],
            [pltpu.HBM((peers * block, LANES), BF), shape_of((8, rows_dev), jnp.int32)],
            scratch=[
                pltpu.VMEM((1, rows_dev), jnp.int32),
                pltpu.VMEM((1, cells), jnp.int32),
                pltpu.VMEM((rows_dev, width), BF),
                pltpu.VMEM((peers * block, LANES), BF),
                pltpu.SemaphoreType.DMA((3,)),
                pltpu.SemaphoreType.DMA((peers,)),
            ],
            flops=2 * slots * rows_dev * width,
            moved=2 * (slots + rows_dev) * width,
        )(cell, cell_place, far(rows))
        got = lax.all_to_all(
            send.reshape(peers, block, LANES), "wide", split_axis=0, concat_axis=0, tiled=False
        ).reshape(peers * block, LANES)
        scored = [score([got], [peers], capacity, coarse, norm, fine_flat)]

    returned = lax.all_to_all(scored[-1][0], "wide", split_axis=0, concat_axis=0, tiled=False)
    coarse_new, fine_new = update(scored, coarse, seed, cells_dev, fine_n)
    row_error = call(
        functools.partial(collect_kernel, peers),
        (),
        [VMEM, VMEM],
        VMEM,
        shape_of((1, rows_dev), F32),
        moved=4 * (8 * rows_dev + peers * LANES),
    )(route, returned).reshape(rows_dev)
    return row_error, coarse_new, fine_new


def solution(mesh):
    in_specs = (
        P(("groups", "wide"), None),
        P(("groups", "wide")),
        P("groups"),
        P(("groups", "wide"), None),
        P(("groups", "wide"), None, None),
        P(("groups", "wide"), None),
    )
    out_specs = (
        P(("groups", "wide")),
        P(("groups", "wide"), None),
        P(("groups", "wide"), None, None),
    )
    return jax.shard_map(shards, mesh=mesh, in_specs=in_specs, out_specs=out_specs, check_vma=False)
```

```python
import functools

import jax
import jax.numpy as jnp
from jax import lax
from jax.experimental import pallas as pl
from jax.experimental.pallas import tpu as pltpu
from jax.sharding import PartitionSpec as P

TEMP = 16
LANES = 128
META = 16
DISTANCES = [8, 1, 12, 2, 9, 3, 13, 4, 10, 5, 14, 6, 11, 7, 15, 0]
WINDOW = 6
VMEM_LIMIT = 24 * 1024 * 1024
BF = jnp.bfloat16
F32 = jnp.float32


def iota(shape, dim):
    return lax.broadcasted_iota(jnp.int32, shape, dim)


def hot(index, size, dtype=BF):
    return (iota((size, index.shape[1]), 0) == index).astype(F32).astype(dtype)


def dot(a, b, dims=((1,), (0,))):
    return lax.dot_general(a, b, (dims, ((), ())), preferred_element_type=F32)


def split3(x):
    high = x.astype(BF)
    rest = x - high.astype(F32)
    mid = rest.astype(BF)
    return high, mid, (rest - mid.astype(F32)).astype(BF)


def put_block(ref, base, rows, meta):
    count, width = rows.shape
    chunks = width // LANES
    whole_rows = count // 16 * 16
    for j in range(chunks):
        ref[base + j * whole_rows : base + (j + 1) * whole_rows, :] = rows[
            :whole_rows, j * LANES : (j + 1) * LANES
        ].astype(BF)
    base += chunks * whole_rows
    if count > whole_rows:
        for j in range(0, chunks, 2):
            pair = [
                rows[whole_rows:, i * LANES : (i + 1) * LANES] for i in (j, j + 1)
            ]
            ref[base : base + 16, :] = jnp.concatenate(pair, axis=0).astype(BF)
            base += 16
    ref[base : base + META, :] = meta


def get_block(ref, base, count, chunks):
    whole_rows = count // 16 * 16
    parts = [
        ref[base + j * whole_rows : base + (j + 1) * whole_rows, :].astype(F32)
        for j in range(chunks)
    ]
    if count > whole_rows:
        base += chunks * whole_rows
        for j in range(0, chunks, 2):
            pair = ref[base + j * 8 : base + j * 8 + 16, :].astype(F32)
            parts[j] = jnp.concatenate([parts[j], pair[:8]], axis=0)
            parts[j + 1] = jnp.concatenate([parts[j + 1], pair[8:]], axis=0)
    return parts


def get_meta(ref, base, count, chunks):
    first = base + chunks * count
    return ref[first : first + META, :].astype(F32)


def find_route(cells_dev, peers, cell_ref, place_ref, upper):
    rows_dev = cell_ref.shape[1]
    cells = place_ref.shape[1]
    cell = cell_ref[...]
    place = place_ref[...]
    table_row = iota((16, cells), 0)
    table = jnp.where(
        table_row == 0, place // cells_dev, jnp.where(table_row == 1, place % cells_dev, 0)
    ).astype(F32).astype(BF)
    found = jnp.zeros((16, rows_dev), F32)
    step = min(cells, 512)
    for first in range(0, cells, step):
        found += dot(table[:, first : first + step], hot(cell - first, step))
    owner = found[0:1].astype(jnp.int32)
    owner_hot = hot(owner, peers, F32)
    running = dot(owner_hot.astype(BF), upper)
    rank = (jnp.sum(running * owner_hot, axis=0, keepdims=True) - 1.0).astype(jnp.int32)
    return owner, found[1:2], rank, owner_hot


def prefix(rows_dev):
    return (iota((rows_dev, rows_dev), 0) <= iota((rows_dev, rows_dev), 1)).astype(F32).astype(BF)


def fetch(sources, targets, sems):
    copies = [
        pltpu.make_async_copy(source, target, sems.at[i])
        for i, (source, target) in enumerate(zip(sources, targets, strict=True))
    ]
    for copy in copies:
        copy.start()
    return copies


def pack_kernel(
    peers, capacity, cells_dev, cell_hbm, place_hbm, rows_hbm,
    send_hbm, route_ref, cell_ref, place_ref, rows_ref, send_ref, in_sems, out_sems,
):
    arrivals = fetch(
        (cell_hbm, place_hbm, rows_hbm), (cell_ref, place_ref, rows_ref), in_sems
    )
    rows_dev, width = rows_ref.shape
    block = (width // LANES) * capacity + META
    upper = prefix(rows_dev)
    arrivals[0].wait()
    arrivals[1].wait()
    owner, local, rank, owner_hot = find_route(cells_dev, peers, cell_ref, place_ref, upper)
    route_ref[...] = jnp.where(iota((8, rows_dev), 0) == 0, owner, rank)
    ids = dot((owner_hot * (local + 1.0)).astype(BF), hot(rank, LANES), ((1,), (1,))).astype(BF)
    slot = owner * capacity + rank
    group = max(1, 256 // capacity)
    arrivals[2].wait()
    departures = []
    for first in range(0, peers, group):
        packed = dot(hot(slot - first * capacity, group * capacity), rows_ref[...])
        for p in range(group):
            put_block(
                send_ref,
                (first + p) * block,
                packed[p * capacity : (p + 1) * capacity],
                jnp.broadcast_to(ids[first + p : first + p + 1], (META, LANES)),
            )
        part = pl.ds(first * block, group * block)
        departures.append(
            pltpu.make_async_copy(
                send_ref.at[part], send_hbm.at[part], out_sems.at[first // group]
            )
        )
        departures[-1].start()
    for copy in departures:
        copy.wait()


def pack_split_kernel(
    peers, capacity, cells_dev, distances, cell_hbm, place_hbm, rows_hbm, *refs
):
    send_hbms = refs[:peers]
    route_ref, cell_ref, place_ref, rows_ref, send_ref, in_sems, out_sems = refs[peers:]
    arrivals = fetch(
        (cell_hbm, place_hbm, rows_hbm), (cell_ref, place_ref, rows_ref), in_sems
    )
    rows_dev, width = rows_ref.shape
    block = (width // LANES) * capacity + META
    upper = prefix(rows_dev)
    me = lax.axis_index("wide")
    arrivals[0].wait()
    arrivals[1].wait()
    owner, local, rank, _ = find_route(cells_dev, peers, cell_ref, place_ref, upper)
    route_ref[...] = jnp.where(iota((8, rows_dev), 0) == 0, owner, rank)
    apart = owner ^ me
    order = jnp.zeros_like(owner)
    for i, r in enumerate(distances):
        order = jnp.where(apart == r, i, order)
    slot = order * capacity + rank
    ids = dot(
        (hot(order, peers, F32) * (local + 1.0)).astype(BF), hot(rank, LANES), ((1,), (1,))
    ).astype(BF)
    group = max(1, 256 // capacity)
    arrivals[2].wait()
    departures = []
    for first in range(0, peers, group):
        packed = dot(hot(slot - first * capacity, group * capacity), rows_ref[...])
        for p in range(group):
            i = first + p
            put_block(
                send_ref,
                i * block,
                packed[p * capacity : (p + 1) * capacity],
                jnp.broadcast_to(ids[i : i + 1], (META, LANES)),
            )
            departures.append(
                pltpu.make_async_copy(
                    send_ref.at[pl.ds(i * block, block)], send_hbms[i], out_sems.at[i]
                )
            )
            departures[-1].start()
    for copy in departures:
        copy.wait()


def seed_kernel(reseed_ref, rows_ref, seed_hbm, seed_ref, sems):
    rows_dev = rows_ref.shape[0]
    part = seed_ref.shape[0] // sems.shape[0]
    copies = []
    for i in range(sems.shape[0]):
        here = slice(i * part, (i + 1) * part)
        picked = hot(reseed_ref[:, here], rows_dev)
        seed_ref[here, :] = dot(picked, rows_ref[...], ((0,), (0,))).astype(BF)
        copies.append(
            pltpu.make_async_copy(seed_ref.at[here], seed_hbm.at[here], sems.at[i])
        )
        copies[-1].start()
    for copy in copies:
        copy.wait()


def score_kernel(blocks, capacity, far_of, known, coarse_ref, norm_ref, fine_ref, *refs):
    got_refs = refs[: len(blocks)]
    known_refs = refs[len(blocks) : len(blocks) + len(known)]
    error_ref, weight_ref, ids_ref, resid_hbm, resid_ref, sems = refs[len(blocks) + len(known) :]
    cells_dev, width = coarse_ref.shape
    fine_n = norm_ref.shape[1]
    chunks = width // LANES
    size = chunks * capacity + META
    group = max(1, 256 // capacity)
    tile = max(1, 512 // fine_n) * fine_n
    places = [(ref, b * size) for ref, count in zip(got_refs, blocks) for b in range(count)]
    error_ref[...] = jnp.zeros_like(error_ref)
    rows_of = list(range(len(places)))
    if far_of is not None:
        me = lax.axis_index("wide")
        rows_of = [me ^ r for r in far_of]
        half = error_ref.shape[0] // 2
        for ref, distances in zip(known_refs, known):
            for i in range(ref.shape[0]):
                row = (me & half) + i if distances is None else me ^ distances[i]
                error_ref[row] = ref[i]
    for p, (ref, base) in enumerate(places):
        ids_ref[:, p * capacity : (p + 1) * capacity] = (
            get_meta(ref, base, capacity, chunks)[0:1, :capacity].astype(jnp.int32) - 1
        )
    norms = split3(norm_ref[...])
    copies = []
    for first in range(0, len(places), group):
        some = places[first : first + group]
        span = len(some) * capacity
        here = slice(first * capacity, first * capacity + span)
        ids = ids_ref[:, here]
        member = hot(ids, cells_dev)
        own = dot(member, coarse_ref[...], ((0,), (0,)))
        square = jnp.zeros((span, LANES), F32)
        got = [get_block(ref, base, capacity, chunks) for ref, base in some]
        for j in range(chunks):
            lanes = slice(j * LANES, (j + 1) * LANES)
            part = (jnp.concatenate([g[j] for g in got], axis=0) - own[:, lanes]).astype(BF)
            resid_ref[here, lanes] = part
            wide = part.astype(F32)
            square += wide * wide
        resid = resid_ref[here, :]
        copies.append(
            pltpu.make_async_copy(resid_ref.at[here], resid_hbm.at[here], sems.at[first // group])
        )
        copies[-1].start()
        column = jnp.sum(square, axis=1, keepdims=True)
        diagonal = iota((span, span), 0) == iota((span, span), 1)
        square_row = jnp.sum(jnp.where(diagonal, column, 0.0), axis=0, keepdims=True)
        best = jnp.zeros((fine_n, span), F32)
        for start in range(0, cells_dev * fine_n, tile):
            scores = dot(fine_ref[start : start + tile, :], resid, ((1,), (1,)))
            for c in range(tile // fine_n):
                best = jnp.where(
                    ids == start // fine_n + c, scores[c * fine_n : (c + 1) * fine_n], best
                )
        norm = sum(dot(part, member, ((0,), (0,))) for part in norms)
        logit = (2.0 * best - norm) * (1.0 / TEMP)
        peak = jnp.max(logit, axis=0, keepdims=True)
        expo = jnp.exp(logit - peak)
        total = jnp.sum(expo, axis=0, keepdims=True)
        weight_ref[:, here] = (expo / total).astype(BF)
        error = square_row - TEMP * (peak + jnp.log(total))
        for p in range(len(some)):
            error_ref[rows_of[first + p], :, :capacity] = error[
                :, p * capacity : (p + 1) * capacity
            ]
    for copy in copies:
        copy.wait()


def update_kernel(sets, coarse_ref, *refs):
    ids_refs, weight_refs, resid_hbms = (refs[i * sets : (i + 1) * sets] for i in range(3))
    (
        seed_hbm, coarse_out_ref, fine_hbm, resid_ref, seed_ref, out_ref, spread_ref, share_ref,
        in_sems, seed_sems, out_sems,
    ) = refs[3 * sets :]
    cells_dev, width = coarse_ref.shape
    fine_n = weight_refs[0].shape[0]
    steps = out_sems.shape[0]
    cells = cells_dev // steps
    rows = cells * fine_n
    starts = [sum(r.shape[0] for r in resid_hbms[:i]) for i in range(sets)]
    arrivals = fetch(
        resid_hbms,
        [resid_ref.at[pl.ds(s, r.shape[0])] for s, r in zip(starts, resid_hbms)],
        in_sems,
    )
    half = seed_ref.shape[0] // 2
    parts = [pl.ds(0, half), pl.ds(half, half)]
    seeds = fetch([seed_hbm.at[p] for p in parts], [seed_ref.at[p] for p in parts], seed_sems)
    ids = jnp.concatenate([ref[...] for ref in ids_refs], axis=1)
    weight = jnp.concatenate([ref[...] for ref in weight_refs], axis=1).astype(F32)
    centre = coarse_ref[...].astype(F32)

    def spread(step):
        for c in range(cells):
            part = jnp.where(ids == step * cells + c, weight, 0.0)
            spread_ref[step % 2, c * fine_n : (c + 1) * fine_n, :] = part.astype(BF)
            first = step * rows + c * fine_n
            share_ref[first : first + fine_n, :] = jnp.broadcast_to(
                1.0 / (jnp.sum(part, axis=1, keepdims=True) + 1.0), (fine_n, LANES)
            )

    def finish(step):
        for c in range(cells):
            here = slice(step * rows + c * fine_n, step * rows + (c + 1) * fine_n)
            own = centre[step * cells + c : step * cells + c + 1]
            share = share_ref[here, :]
            for j in range(0, width, LANES):
                lanes = slice(j, j + LANES)
                seed = seed_ref[here, lanes].astype(F32) - own[:, lanes]
                out_ref[here, lanes] = (out_ref[here, lanes] + seed) * share
        part = pl.ds(step * rows, rows)
        copy = pltpu.make_async_copy(out_ref.at[part], fine_hbm.at[part], out_sems.at[step])
        copy.start()
        return copy

    spread(0)
    for copy in arrivals:
        copy.wait()
    departures = []
    for step in range(steps + 1):
        if step == 1:
            seeds[0].wait()
        if step == steps // 2 + 1:
            seeds[1].wait()
        if step < steps:
            out_ref[step * rows : (step + 1) * rows, :] = dot(spread_ref[step % 2], resid_ref[...])
        if step + 1 < steps:
            spread(step + 1)
        if step > 0:
            departures.append(finish(step - 1))
    member = hot(ids, cells_dev, F32)
    count = jnp.sum(member, axis=1, keepdims=True)
    coarse_out_ref[...] = centre + dot(member.astype(BF), resid_ref[...]) / (count + 1.0)
    for copy in departures:
        copy.wait()


def collect_kernel(peers, route_ref, error_ref, out_ref):
    owner_hot = hot(route_ref[0:1, :], peers, F32)
    rank_hot = hot(route_ref[1:2, :], LANES)
    error = error_ref[...].reshape(peers, LANES)
    picked = sum(dot(part, rank_hot) for part in split3(error))
    out_ref[...] = jnp.sum(picked * owner_hot, axis=0, keepdims=True)


def far(x):
    return pltpu.with_memory_space_constraint(x, pltpu.HBM)


def whole(shape):
    return pl.BlockSpec(shape, lambda *_: (0,) * len(shape))


HBM = pl.BlockSpec(memory_space=pltpu.HBM)
VMEM = pl.BlockSpec(memory_space=pltpu.VMEM)


def call(kernel, grid, in_specs, out_specs, out_shape, scratch=(), flops=0, moved=0):
    return pl.pallas_call(
        kernel,
        grid=grid,
        in_specs=in_specs,
        out_specs=out_specs,
        out_shape=out_shape,
        scratch_shapes=scratch,
        compiler_params=pltpu.CompilerParams(vmem_limit_bytes=VMEM_LIMIT),
        cost_estimate=pl.CostEstimate(flops=flops, bytes_accessed=moved, transcendentals=0),
    )


def shape_of(shape, dtype):
    return jax.ShapeDtypeStruct(shape, dtype)


def score(got, blocks, capacity, coarse, norm, fine, far_of=None, known=(), errors=(), peers=0):
    width = coarse.shape[1]
    fine_n = norm.shape[1]
    count = sum(blocks)
    slots = count * capacity
    return call(
        functools.partial(score_kernel, blocks, capacity, far_of, known),
        (),
        [VMEM] * (3 + len(got) + len(errors)),
        [VMEM, VMEM, VMEM, HBM],
        [
            shape_of((peers or count, 1, LANES), F32),
            shape_of((fine_n, slots), BF),
            shape_of((1, slots), jnp.int32),
            pltpu.HBM((slots, width), BF),
        ],
        scratch=[
            pltpu.VMEM((slots, width), BF),
            pltpu.SemaphoreType.DMA((count,)),
        ],
        flops=2 * slots * fine.shape[0] * width,
        moved=2 * (2 * slots + fine.shape[0]) * width,
    )(coarse, norm, fine, *got, *errors)


def update(scored, coarse, seed, cells_dev, fine_n):
    width = coarse.shape[1]
    fine_all = cells_dev * fine_n
    sets = len(scored)
    _, weights, ids, resids = zip(*scored)
    slots = sum(r.shape[0] for r in resids)
    steps = max(2, cells_dev // 4)
    coarse_new, fine_new = call(
        functools.partial(update_kernel, sets),
        (),
        [VMEM] * (1 + 2 * sets) + [HBM] * (sets + 1),
        [VMEM, HBM],
        [shape_of((cells_dev, width), F32), pltpu.HBM((fine_all, width), F32)],
        scratch=[
            pltpu.VMEM((slots, width), BF),
            pltpu.VMEM((fine_all, width), BF),
            pltpu.VMEM((fine_all, width), F32),
            pltpu.VMEM((2, fine_all // steps, slots), BF),
            pltpu.VMEM((fine_all, LANES), F32),
            pltpu.SemaphoreType.DMA((sets,)),
            pltpu.SemaphoreType.DMA((2,)),
            pltpu.SemaphoreType.DMA((steps,)),
        ],
        flops=2 * slots * fine_all * width,
        moved=2 * slots * width + 6 * fine_all * width,
    )(coarse, *ids, *weights, *[far(r) for r in resids], far(seed))
    return coarse_new, fine_new.reshape(cells_dev, fine_n, width)


def shards(rows, cell, cell_place, coarse, fine, reseed):
    peers = lax.axis_size("wide")
    rows_dev, width = rows.shape
    cells_dev, fine_n, _ = fine.shape
    cells = cell_place.shape[0]
    capacity = max(16, 2 * rows_dev // peers)
    slots = peers * capacity
    block = (width // LANES) * capacity + META
    fine_all = cells_dev * fine_n

    fine_wide = fine.astype(F32)
    norm = jnp.sum(fine_wide * fine_wide, axis=-1)
    fine_flat = fine.reshape(fine_all, width)
    seed = call(
        seed_kernel,
        (),
        [VMEM, VMEM],
        HBM,
        pltpu.HBM((fine_all, width), BF),
        scratch=[pltpu.VMEM((fine_all, width), BF), pltpu.SemaphoreType.DMA((4,))],
        flops=2 * fine_all * rows_dev * width,
        moved=2 * (fine_all + rows_dev) * width,
    )(reseed.reshape(1, fine_all), rows)
    cell = far(cell.reshape(1, rows_dev))
    cell_place = far(cell_place.reshape(1, cells))
    if capacity == 64 and peers == 16:
        distances = DISTANCES
        *sends, route = call(
            functools.partial(pack_split_kernel, peers, capacity, cells_dev, distances),
            (),
            [HBM] * 3,
            [HBM] * peers + [VMEM],
            [pltpu.HBM((block, LANES), BF)] * peers + [shape_of((8, rows_dev), jnp.int32)],
            scratch=[
                pltpu.VMEM((1, rows_dev), jnp.int32),
                pltpu.VMEM((1, cells), jnp.int32),
                pltpu.VMEM((rows_dev, width), BF),
                pltpu.VMEM((peers * block, LANES), BF),
                pltpu.SemaphoreType.DMA((3,)),
                pltpu.SemaphoreType.DMA((peers,)),
            ],
            flops=2 * slots * rows_dev * width,
            moved=2 * (slots + 2 * rows_dev) * width,
        )(cell, cell_place, far(rows))
        got = []
        for i, r in enumerate(distances):
            block_out = sends[i]
            if i >= WINDOW:
                block_out, got[i - WINDOW] = lax.optimization_barrier((block_out, got[i - WINDOW]))
            if r:
                block_out = lax.ppermute(block_out, "wide", [(p, p ^ r) for p in range(peers)])
            got.append(block_out)
        tables = (coarse, norm, fine_flat)
        scored = []
        for first in range(0, peers, 4):
            some = got[first : first + 4]
            if first + 4 < peers:
                scored.append(score(some, [1] * 4, capacity, *tables))
            else:
                known = tuple(distances[i : i + 4] for i in range(0, first, 4))
                errors = [x[0] for x in scored]
                scored.append(
                    score(some, [1] * 4, capacity, *tables, distances[first:], known, errors, peers)
                )
    else:
        send, route = call(
            functools.partial(pack_kernel, peers, capacity, cells_dev),
            (),
            [HBM] * 3,
            [HBM, VMEM],
            [pltpu.HBM((peers * block, LANES), BF), shape_of((8, rows_dev), jnp.int32)],
            scratch=[
                pltpu.VMEM((1, rows_dev), jnp.int32),
                pltpu.VMEM((1, cells), jnp.int32),
                pltpu.VMEM((rows_dev, width), BF),
                pltpu.VMEM((peers * block, LANES), BF),
                pltpu.SemaphoreType.DMA((3,)),
                pltpu.SemaphoreType.DMA((peers,)),
            ],
            flops=2 * slots * rows_dev * width,
            moved=2 * (slots + rows_dev) * width,
        )(cell, cell_place, far(rows))
        got = lax.all_to_all(
            send.reshape(peers, block, LANES), "wide", split_axis=0, concat_axis=0, tiled=False
        ).reshape(peers * block, LANES)
        scored = [score([got], [peers], capacity, coarse, norm, fine_flat)]

    returned = lax.all_to_all(scored[-1][0], "wide", split_axis=0, concat_axis=0, tiled=False)
    coarse_new, fine_new = update(scored, coarse, seed, cells_dev, fine_n)
    row_error = call(
        functools.partial(collect_kernel, peers),
        (),
        [VMEM, VMEM],
        VMEM,
        shape_of((1, rows_dev), F32),
        moved=4 * (8 * rows_dev + peers * LANES),
    )(route, returned).reshape(rows_dev)
    return row_error, coarse_new, fine_new


def solution(mesh):
    in_specs = (
        P(("groups", "wide"), None),
        P(("groups", "wide")),
        P("groups"),
        P(("groups", "wide"), None),
        P(("groups", "wide"), None, None),
        P(("groups", "wide"), None),
    )
    out_specs = (
        P(("groups", "wide")),
        P(("groups", "wide"), None),
        P(("groups", "wide"), None, None),
    )
    return jax.shard_map(shards, mesh=mesh, in_specs=in_specs, out_specs=out_specs, check_vma=False)
```

```python
import functools

import jax
import jax.numpy as jnp
from jax import lax
from jax.experimental import pallas as pl
from jax.experimental.pallas import tpu as pltpu
from jax.sharding import PartitionSpec as P

TEMP = 16
LANES = 128
META = 16
DISTANCES = [8, 7, 12, 6, 10, 5, 14, 4, 9, 3, 13, 2, 11, 1, 15, 0]
WINDOW = 6
SIZES = (4, 4, 6, 2)
VMEM_LIMIT = 24 * 1024 * 1024
BF = jnp.bfloat16
F32 = jnp.float32


def iota(shape, dim):
    return lax.broadcasted_iota(jnp.int32, shape, dim)


def hot(index, size, dtype=BF):
    return (iota((size, index.shape[1]), 0) == index).astype(F32).astype(dtype)


def dot(a, b, dims=((1,), (0,))):
    return lax.dot_general(a, b, (dims, ((), ())), preferred_element_type=F32)


def split3(x):
    high = x.astype(BF)
    rest = x - high.astype(F32)
    mid = rest.astype(BF)
    return high, mid, (rest - mid.astype(F32)).astype(BF)


def put_block(ref, base, rows, meta):
    count, width = rows.shape
    chunks = width // LANES
    whole_rows = count // 16 * 16
    for j in range(chunks):
        ref[base + j * whole_rows : base + (j + 1) * whole_rows, :] = rows[
            :whole_rows, j * LANES : (j + 1) * LANES
        ].astype(BF)
    base += chunks * whole_rows
    if count > whole_rows:
        for j in range(0, chunks, 2):
            pair = [
                rows[whole_rows:, i * LANES : (i + 1) * LANES] for i in (j, j + 1)
            ]
            ref[base : base + 16, :] = jnp.concatenate(pair, axis=0).astype(BF)
            base += 16
    ref[base : base + META, :] = meta


def get_block(ref, base, count, chunks):
    whole_rows = count // 16 * 16
    parts = [
        ref[base + j * whole_rows : base + (j + 1) * whole_rows, :].astype(F32)
        for j in range(chunks)
    ]
    if count > whole_rows:
        base += chunks * whole_rows
        for j in range(0, chunks, 2):
            pair = ref[base + j * 8 : base + j * 8 + 16, :].astype(F32)
            parts[j] = jnp.concatenate([parts[j], pair[:8]], axis=0)
            parts[j + 1] = jnp.concatenate([parts[j + 1], pair[8:]], axis=0)
    return parts


def get_meta(ref, base, count, chunks):
    first = base + chunks * count
    return ref[first : first + META, :].astype(F32)


def find_route(cells_dev, peers, cell_ref, place_ref, upper):
    rows_dev = cell_ref.shape[1]
    cells = place_ref.shape[1]
    cell = cell_ref[...]
    place = place_ref[...]
    table_row = iota((16, cells), 0)
    table = jnp.where(
        table_row == 0, place // cells_dev, jnp.where(table_row == 1, place % cells_dev, 0)
    ).astype(F32).astype(BF)
    found = jnp.zeros((16, rows_dev), F32)
    step = min(cells, 512)
    for first in range(0, cells, step):
        found += dot(table[:, first : first + step], hot(cell - first, step))
    owner = found[0:1].astype(jnp.int32)
    owner_hot = hot(owner, peers, F32)
    running = dot(owner_hot.astype(BF), upper)
    rank = (jnp.sum(running * owner_hot, axis=0, keepdims=True) - 1.0).astype(jnp.int32)
    return owner, found[1:2], rank, owner_hot


def prefix(rows_dev):
    return (iota((rows_dev, rows_dev), 0) <= iota((rows_dev, rows_dev), 1)).astype(F32).astype(BF)


def fetch(sources, targets, sems):
    copies = [
        pltpu.make_async_copy(source, target, sems.at[i])
        for i, (source, target) in enumerate(zip(sources, targets, strict=True))
    ]
    for copy in copies:
        copy.start()
    return copies


def pack_kernel(
    peers, capacity, cells_dev, cell_hbm, place_hbm, rows_hbm,
    send_hbm, route_ref, cell_ref, place_ref, rows_ref, send_ref, in_sems, out_sems,
):
    arrivals = fetch(
        (cell_hbm, place_hbm, rows_hbm), (cell_ref, place_ref, rows_ref), in_sems
    )
    rows_dev, width = rows_ref.shape
    block = (width // LANES) * capacity + META
    upper = prefix(rows_dev)
    arrivals[0].wait()
    arrivals[1].wait()
    owner, local, rank, owner_hot = find_route(cells_dev, peers, cell_ref, place_ref, upper)
    route_ref[...] = jnp.where(iota((8, rows_dev), 0) == 0, owner, rank)
    ids = dot((owner_hot * (local + 1.0)).astype(BF), hot(rank, LANES), ((1,), (1,))).astype(BF)
    slot = owner * capacity + rank
    group = max(1, 256 // capacity)
    arrivals[2].wait()
    departures = []
    for first in range(0, peers, group):
        packed = dot(hot(slot - first * capacity, group * capacity), rows_ref[...])
        for p in range(group):
            put_block(
                send_ref,
                (first + p) * block,
                packed[p * capacity : (p + 1) * capacity],
                jnp.broadcast_to(ids[first + p : first + p + 1], (META, LANES)),
            )
        part = pl.ds(first * block, group * block)
        departures.append(
            pltpu.make_async_copy(
                send_ref.at[part], send_hbm.at[part], out_sems.at[first // group]
            )
        )
        departures[-1].start()
    for copy in departures:
        copy.wait()


def pack_split_kernel(
    peers, capacity, cells_dev, distances, cell_hbm, place_hbm, rows_hbm, *refs
):
    send_hbms = refs[:peers]
    route_ref, cell_ref, place_ref, rows_ref, send_ref, in_sems, out_sems = refs[peers:]
    arrivals = fetch(
        (cell_hbm, place_hbm, rows_hbm), (cell_ref, place_ref, rows_ref), in_sems
    )
    rows_dev, width = rows_ref.shape
    block = (width // LANES) * capacity + META
    upper = prefix(rows_dev)
    me = lax.axis_index("wide")
    arrivals[0].wait()
    arrivals[1].wait()
    owner, local, rank, _ = find_route(cells_dev, peers, cell_ref, place_ref, upper)
    route_ref[...] = jnp.where(iota((8, rows_dev), 0) == 0, owner, rank)
    apart = owner ^ me
    order = jnp.zeros_like(owner)
    for i, r in enumerate(distances):
        order = jnp.where(apart == r, i, order)
    slot = order * capacity + rank
    ids = dot(
        (hot(order, peers, F32) * (local + 1.0)).astype(BF), hot(rank, LANES), ((1,), (1,))
    ).astype(BF)
    group = max(1, 256 // capacity)
    arrivals[2].wait()
    departures = []
    for first in range(0, peers, group):
        packed = dot(hot(slot - first * capacity, group * capacity), rows_ref[...])
        for p in range(group):
            i = first + p
            put_block(
                send_ref,
                i * block,
                packed[p * capacity : (p + 1) * capacity],
                jnp.broadcast_to(ids[i : i + 1], (META, LANES)),
            )
            departures.append(
                pltpu.make_async_copy(
                    send_ref.at[pl.ds(i * block, block)], send_hbms[i], out_sems.at[i]
                )
            )
            departures[-1].start()
    for copy in departures:
        copy.wait()


def seed_kernel(reseed_ref, rows_ref, seed_hbm, seed_ref, sems):
    rows_dev = rows_ref.shape[0]
    part = seed_ref.shape[0] // sems.shape[0]
    copies = []
    for i in range(sems.shape[0]):
        here = slice(i * part, (i + 1) * part)
        picked = hot(reseed_ref[:, here], rows_dev)
        seed_ref[here, :] = dot(picked, rows_ref[...], ((0,), (0,))).astype(BF)
        copies.append(
            pltpu.make_async_copy(seed_ref.at[here], seed_hbm.at[here], sems.at[i])
        )
        copies[-1].start()
    for copy in copies:
        copy.wait()


def score_kernel(blocks, capacity, far_of, known, coarse_ref, norm_ref, fine_ref, *refs):
    got_refs = refs[: len(blocks)]
    known_refs = refs[len(blocks) : len(blocks) + len(known)]
    error_ref, weight_ref, ids_ref, resid_hbm, resid_ref, sems = refs[len(blocks) + len(known) :]
    cells_dev, width = coarse_ref.shape
    fine_n = norm_ref.shape[1]
    chunks = width // LANES
    size = chunks * capacity + META
    group = max(1, 256 // capacity)
    tile = max(1, 512 // fine_n) * fine_n
    places = [(ref, b * size) for ref, count in zip(got_refs, blocks) for b in range(count)]
    error_ref[...] = jnp.zeros_like(error_ref)
    rows_of = list(range(len(places)))
    if far_of is not None:
        me = lax.axis_index("wide")
        rows_of = [me ^ r for r in far_of]
        half = error_ref.shape[0] // 2
        for ref, distances in zip(known_refs, known):
            for i in range(ref.shape[0]):
                row = (me & half) + i if distances is None else me ^ distances[i]
                error_ref[row] = ref[i]
    for p, (ref, base) in enumerate(places):
        ids_ref[:, p * capacity : (p + 1) * capacity] = (
            get_meta(ref, base, capacity, chunks)[0:1, :capacity].astype(jnp.int32) - 1
        )
    norms = split3(norm_ref[...])
    copies = []
    for first in range(0, len(places), group):
        some = places[first : first + group]
        span = len(some) * capacity
        here = slice(first * capacity, first * capacity + span)
        ids = ids_ref[:, here]
        member = hot(ids, cells_dev)
        own = dot(member, coarse_ref[...], ((0,), (0,)))
        square = jnp.zeros((span, LANES), F32)
        got = [get_block(ref, base, capacity, chunks) for ref, base in some]
        for j in range(chunks):
            lanes = slice(j * LANES, (j + 1) * LANES)
            part = (jnp.concatenate([g[j] for g in got], axis=0) - own[:, lanes]).astype(BF)
            resid_ref[here, lanes] = part
            wide = part.astype(F32)
            square += wide * wide
        resid = resid_ref[here, :]
        copies.append(
            pltpu.make_async_copy(resid_ref.at[here], resid_hbm.at[here], sems.at[first // group])
        )
        copies[-1].start()
        column = jnp.sum(square, axis=1, keepdims=True)
        diagonal = iota((span, span), 0) == iota((span, span), 1)
        square_row = jnp.sum(jnp.where(diagonal, column, 0.0), axis=0, keepdims=True)
        best = jnp.zeros((fine_n, span), F32)
        for start in range(0, cells_dev * fine_n, tile):
            scores = dot(fine_ref[start : start + tile, :], resid, ((1,), (1,)))
            for c in range(tile // fine_n):
                best = jnp.where(
                    ids == start // fine_n + c, scores[c * fine_n : (c + 1) * fine_n], best
                )
        norm = sum(dot(part, member, ((0,), (0,))) for part in norms)
        logit = (2.0 * best - norm) * (1.0 / TEMP)
        peak = jnp.max(logit, axis=0, keepdims=True)
        expo = jnp.exp(logit - peak)
        total = jnp.sum(expo, axis=0, keepdims=True)
        weight_ref[:, here] = (expo / total).astype(BF)
        error = square_row - TEMP * (peak + jnp.log(total))
        for p in range(len(some)):
            error_ref[rows_of[first + p], :, :capacity] = error[
                :, p * capacity : (p + 1) * capacity
            ]
    for copy in copies:
        copy.wait()


def update_kernel(sets, coarse_ref, *refs):
    ids_refs, weight_refs, resid_hbms = (refs[i * sets : (i + 1) * sets] for i in range(3))
    (
        seed_hbm, coarse_out_ref, fine_hbm, resid_ref, seed_ref, out_ref, spread_ref, share_ref,
        in_sems, seed_sems, out_sems,
    ) = refs[3 * sets :]
    cells_dev, width = coarse_ref.shape
    fine_n = weight_refs[0].shape[0]
    steps = out_sems.shape[0]
    cells = cells_dev // steps
    rows = cells * fine_n
    starts = [sum(r.shape[0] for r in resid_hbms[:i]) for i in range(sets)]
    arrivals = fetch(
        resid_hbms,
        [resid_ref.at[pl.ds(s, r.shape[0])] for s, r in zip(starts, resid_hbms)],
        in_sems,
    )
    half = seed_ref.shape[0] // 2
    parts = [pl.ds(0, half), pl.ds(half, half)]
    seeds = fetch([seed_hbm.at[p] for p in parts], [seed_ref.at[p] for p in parts], seed_sems)
    ids = jnp.concatenate([ref[...] for ref in ids_refs], axis=1)
    weight = jnp.concatenate([ref[...] for ref in weight_refs], axis=1).astype(F32)
    centre = coarse_ref[...].astype(F32)

    def spread(step):
        for c in range(cells):
            part = jnp.where(ids == step * cells + c, weight, 0.0)
            spread_ref[step % 2, c * fine_n : (c + 1) * fine_n, :] = part.astype(BF)
            first = step * rows + c * fine_n
            share_ref[first : first + fine_n, :] = jnp.broadcast_to(
                1.0 / (jnp.sum(part, axis=1, keepdims=True) + 1.0), (fine_n, LANES)
            )

    def finish(step):
        for c in range(cells):
            here = slice(step * rows + c * fine_n, step * rows + (c + 1) * fine_n)
            own = centre[step * cells + c : step * cells + c + 1]
            share = share_ref[here, :]
            for j in range(0, width, LANES):
                lanes = slice(j, j + LANES)
                seed = seed_ref[here, lanes].astype(F32) - own[:, lanes]
                out_ref[here, lanes] = (out_ref[here, lanes] + seed) * share
        part = pl.ds(step * rows, rows)
        copy = pltpu.make_async_copy(out_ref.at[part], fine_hbm.at[part], out_sems.at[step])
        copy.start()
        return copy

    spread(0)
    for copy in arrivals:
        copy.wait()
    departures = []
    for step in range(steps + 1):
        if step == 1:
            seeds[0].wait()
        if step == steps // 2 + 1:
            seeds[1].wait()
        if step < steps:
            out_ref[step * rows : (step + 1) * rows, :] = dot(spread_ref[step % 2], resid_ref[...])
        if step + 1 < steps:
            spread(step + 1)
        if step > 0:
            departures.append(finish(step - 1))
    member = hot(ids, cells_dev, F32)
    count = jnp.sum(member, axis=1, keepdims=True)
    coarse_out_ref[...] = centre + dot(member.astype(BF), resid_ref[...]) / (count + 1.0)
    for copy in departures:
        copy.wait()


def collect_kernel(peers, route_ref, error_ref, out_ref):
    owner_hot = hot(route_ref[0:1, :], peers, F32)
    rank_hot = hot(route_ref[1:2, :], LANES)
    error = error_ref[...].reshape(peers, LANES)
    picked = sum(dot(part, rank_hot) for part in split3(error))
    out_ref[...] = jnp.sum(picked * owner_hot, axis=0, keepdims=True)


def far(x):
    return pltpu.with_memory_space_constraint(x, pltpu.HBM)


def whole(shape):
    return pl.BlockSpec(shape, lambda *_: (0,) * len(shape))


HBM = pl.BlockSpec(memory_space=pltpu.HBM)
VMEM = pl.BlockSpec(memory_space=pltpu.VMEM)


def call(kernel, grid, in_specs, out_specs, out_shape, scratch=(), flops=0, moved=0):
    return pl.pallas_call(
        kernel,
        grid=grid,
        in_specs=in_specs,
        out_specs=out_specs,
        out_shape=out_shape,
        scratch_shapes=scratch,
        compiler_params=pltpu.CompilerParams(vmem_limit_bytes=VMEM_LIMIT),
        cost_estimate=pl.CostEstimate(flops=flops, bytes_accessed=moved, transcendentals=0),
    )


def shape_of(shape, dtype):
    return jax.ShapeDtypeStruct(shape, dtype)


def score(got, blocks, capacity, coarse, norm, fine, far_of=None, known=(), errors=(), peers=0):
    width = coarse.shape[1]
    fine_n = norm.shape[1]
    count = sum(blocks)
    slots = count * capacity
    return call(
        functools.partial(score_kernel, blocks, capacity, far_of, known),
        (),
        [VMEM] * (3 + len(got) + len(errors)),
        [VMEM, VMEM, VMEM, HBM],
        [
            shape_of((peers or count, 1, LANES), F32),
            shape_of((fine_n, slots), BF),
            shape_of((1, slots), jnp.int32),
            pltpu.HBM((slots, width), BF),
        ],
        scratch=[
            pltpu.VMEM((slots, width), BF),
            pltpu.SemaphoreType.DMA((count,)),
        ],
        flops=2 * slots * fine.shape[0] * width,
        moved=2 * (2 * slots + fine.shape[0]) * width,
    )(coarse, norm, fine, *got, *errors)


def update(scored, coarse, seed, cells_dev, fine_n):
    width = coarse.shape[1]
    fine_all = cells_dev * fine_n
    sets = len(scored)
    _, weights, ids, resids = zip(*scored)
    slots = sum(r.shape[0] for r in resids)
    steps = max(2, cells_dev // 4)
    coarse_new, fine_new = call(
        functools.partial(update_kernel, sets),
        (),
        [VMEM] * (1 + 2 * sets) + [HBM] * (sets + 1),
        [VMEM, HBM],
        [shape_of((cells_dev, width), F32), pltpu.HBM((fine_all, width), F32)],
        scratch=[
            pltpu.VMEM((slots, width), BF),
            pltpu.VMEM((fine_all, width), BF),
            pltpu.VMEM((fine_all, width), F32),
            pltpu.VMEM((2, fine_all // steps, slots), BF),
            pltpu.VMEM((fine_all, LANES), F32),
            pltpu.SemaphoreType.DMA((sets,)),
            pltpu.SemaphoreType.DMA((2,)),
            pltpu.SemaphoreType.DMA((steps,)),
        ],
        flops=2 * slots * fine_all * width,
        moved=2 * slots * width + 6 * fine_all * width,
    )(coarse, *ids, *weights, *[far(r) for r in resids], far(seed))
    return coarse_new, fine_new.reshape(cells_dev, fine_n, width)


def shards(rows, cell, cell_place, coarse, fine, reseed):
    peers = lax.axis_size("wide")
    rows_dev, width = rows.shape
    cells_dev, fine_n, _ = fine.shape
    cells = cell_place.shape[0]
    capacity = max(16, 2 * rows_dev // peers)
    slots = peers * capacity
    block = (width // LANES) * capacity + META
    fine_all = cells_dev * fine_n

    fine_wide = fine.astype(F32)
    norm = jnp.sum(fine_wide * fine_wide, axis=-1)
    fine_flat = fine.reshape(fine_all, width)
    seed = call(
        seed_kernel,
        (),
        [VMEM, VMEM],
        HBM,
        pltpu.HBM((fine_all, width), BF),
        scratch=[pltpu.VMEM((fine_all, width), BF), pltpu.SemaphoreType.DMA((4,))],
        flops=2 * fine_all * rows_dev * width,
        moved=2 * (fine_all + rows_dev) * width,
    )(reseed.reshape(1, fine_all), rows)
    cell = far(cell.reshape(1, rows_dev))
    cell_place = far(cell_place.reshape(1, cells))
    if capacity == 64 and peers == 16:
        distances = DISTANCES
        *sends, route = call(
            functools.partial(pack_split_kernel, peers, capacity, cells_dev, distances),
            (),
            [HBM] * 3,
            [HBM] * peers + [VMEM],
            [pltpu.HBM((block, LANES), BF)] * peers + [shape_of((8, rows_dev), jnp.int32)],
            scratch=[
                pltpu.VMEM((1, rows_dev), jnp.int32),
                pltpu.VMEM((1, cells), jnp.int32),
                pltpu.VMEM((rows_dev, width), BF),
                pltpu.VMEM((peers * block, LANES), BF),
                pltpu.SemaphoreType.DMA((3,)),
                pltpu.SemaphoreType.DMA((peers,)),
            ],
            flops=2 * slots * rows_dev * width,
            moved=2 * (slots + 2 * rows_dev) * width,
        )(cell, cell_place, far(rows))
        got = []
        for i, r in enumerate(distances):
            block_out = sends[i]
            if i >= WINDOW:
                block_out, got[i - WINDOW] = lax.optimization_barrier((block_out, got[i - WINDOW]))
            if r:
                block_out = lax.ppermute(block_out, "wide", [(p, p ^ r) for p in range(peers)])
            got.append(block_out)
        tables = (coarse, norm, fine_flat)
        scored = []
        for size in SIZES:
            first = sum(SIZES[: len(scored)])
            some = got[first : first + size]
            if first + size < peers:
                scored.append(score(some, [1] * size, capacity, *tables))
            else:
                ends = [sum(SIZES[: i + 1]) for i in range(len(scored))]
                known = tuple(distances[e - n : e] for e, n in zip(ends, SIZES))
                errors = [x[0] for x in scored]
                scored.append(
                    score(
                        some, [1] * size, capacity, *tables, distances[first:], known, errors, peers
                    )
                )
    else:
        send, route = call(
            functools.partial(pack_kernel, peers, capacity, cells_dev),
            (),
            [HBM] * 3,
            [HBM, VMEM],
            [pltpu.HBM((peers * block, LANES), BF), shape_of((8, rows_dev), jnp.int32)],
            scratch=[
                pltpu.VMEM((1, rows_dev), jnp.int32),
                pltpu.VMEM((1, cells), jnp.int32),
                pltpu.VMEM((rows_dev, width), BF),
                pltpu.VMEM((peers * block, LANES), BF),
                pltpu.SemaphoreType.DMA((3,)),
                pltpu.SemaphoreType.DMA((peers,)),
            ],
            flops=2 * slots * rows_dev * width,
            moved=2 * (slots + rows_dev) * width,
        )(cell, cell_place, far(rows))
        got = lax.all_to_all(
            send.reshape(peers, block, LANES), "wide", split_axis=0, concat_axis=0, tiled=False
        ).reshape(peers * block, LANES)
        scored = [score([got], [peers], capacity, coarse, norm, fine_flat)]

    returned = lax.all_to_all(scored[-1][0], "wide", split_axis=0, concat_axis=0, tiled=False)
    coarse_new, fine_new = update(scored, coarse, seed, cells_dev, fine_n)
    row_error = call(
        functools.partial(collect_kernel, peers),
        (),
        [VMEM, VMEM],
        VMEM,
        shape_of((1, rows_dev), F32),
        moved=4 * (8 * rows_dev + peers * LANES),
    )(route, returned).reshape(rows_dev)
    return row_error, coarse_new, fine_new


def solution(mesh):
    in_specs = (
        P(("groups", "wide"), None),
        P(("groups", "wide")),
        P("groups"),
        P(("groups", "wide"), None),
        P(("groups", "wide"), None, None),
        P(("groups", "wide"), None),
    )
    out_specs = (
        P(("groups", "wide")),
        P(("groups", "wide"), None),
        P(("groups", "wide"), None, None),
    )
    return jax.shard_map(shards, mesh=mesh, in_specs=in_specs, out_specs=out_specs, check_vma=False)
```

```python
import functools

import jax
import jax.numpy as jnp
from jax import lax
from jax.experimental import pallas as pl
from jax.experimental.pallas import tpu as pltpu
from jax.sharding import PartitionSpec as P

TEMP = 16
LANES = 128
META = 16
DISTANCES = [10, 7, 14, 6, 8, 5, 12, 4, 11, 3, 15, 2, 9, 1, 13, 0]
WINDOW = 6
SIZES = (4, 4, 6, 2)
VMEM_LIMIT = 24 * 1024 * 1024
BF = jnp.bfloat16
F32 = jnp.float32


def iota(shape, dim):
    return lax.broadcasted_iota(jnp.int32, shape, dim)


def hot(index, size, dtype=BF):
    return (iota((size, index.shape[1]), 0) == index).astype(F32).astype(dtype)


def dot(a, b, dims=((1,), (0,))):
    return lax.dot_general(a, b, (dims, ((), ())), preferred_element_type=F32)


def split3(x):
    high = x.astype(BF)
    rest = x - high.astype(F32)
    mid = rest.astype(BF)
    return high, mid, (rest - mid.astype(F32)).astype(BF)


def put_block(ref, base, rows, meta):
    count, width = rows.shape
    chunks = width // LANES
    whole_rows = count // 16 * 16
    for j in range(chunks):
        ref[base + j * whole_rows : base + (j + 1) * whole_rows, :] = rows[
            :whole_rows, j * LANES : (j + 1) * LANES
        ].astype(BF)
    base += chunks * whole_rows
    if count > whole_rows:
        for j in range(0, chunks, 2):
            pair = [
                rows[whole_rows:, i * LANES : (i + 1) * LANES] for i in (j, j + 1)
            ]
            ref[base : base + 16, :] = jnp.concatenate(pair, axis=0).astype(BF)
            base += 16
    ref[base : base + META, :] = meta


def get_block(ref, base, count, chunks):
    whole_rows = count // 16 * 16
    parts = [
        ref[base + j * whole_rows : base + (j + 1) * whole_rows, :].astype(F32)
        for j in range(chunks)
    ]
    if count > whole_rows:
        base += chunks * whole_rows
        for j in range(0, chunks, 2):
            pair = ref[base + j * 8 : base + j * 8 + 16, :].astype(F32)
            parts[j] = jnp.concatenate([parts[j], pair[:8]], axis=0)
            parts[j + 1] = jnp.concatenate([parts[j + 1], pair[8:]], axis=0)
    return parts


def get_meta(ref, base, count, chunks):
    first = base + chunks * count
    return ref[first : first + META, :].astype(F32)


def find_route(cells_dev, peers, cell_ref, place_ref, upper):
    rows_dev = cell_ref.shape[1]
    cells = place_ref.shape[1]
    cell = cell_ref[...]
    place = place_ref[...]
    table_row = iota((16, cells), 0)
    table = jnp.where(
        table_row == 0, place // cells_dev, jnp.where(table_row == 1, place % cells_dev, 0)
    ).astype(F32).astype(BF)
    found = jnp.zeros((16, rows_dev), F32)
    step = min(cells, 512)
    for first in range(0, cells, step):
        found += dot(table[:, first : first + step], hot(cell - first, step))
    owner = found[0:1].astype(jnp.int32)
    owner_hot = hot(owner, peers, F32)
    running = dot(owner_hot.astype(BF), upper)
    rank = (jnp.sum(running * owner_hot, axis=0, keepdims=True) - 1.0).astype(jnp.int32)
    return owner, found[1:2], rank, owner_hot


def prefix(rows_dev):
    return (iota((rows_dev, rows_dev), 0) <= iota((rows_dev, rows_dev), 1)).astype(F32).astype(BF)


def fetch(sources, targets, sems):
    copies = [
        pltpu.make_async_copy(source, target, sems.at[i])
        for i, (source, target) in enumerate(zip(sources, targets, strict=True))
    ]
    for copy in copies:
        copy.start()
    return copies


def pack_kernel(
    peers, capacity, cells_dev, cell_hbm, place_hbm, rows_hbm,
    send_hbm, route_ref, cell_ref, place_ref, rows_ref, send_ref, in_sems, out_sems,
):
    arrivals = fetch(
        (cell_hbm, place_hbm, rows_hbm), (cell_ref, place_ref, rows_ref), in_sems
    )
    rows_dev, width = rows_ref.shape
    block = (width // LANES) * capacity + META
    upper = prefix(rows_dev)
    arrivals[0].wait()
    arrivals[1].wait()
    owner, local, rank, owner_hot = find_route(cells_dev, peers, cell_ref, place_ref, upper)
    route_ref[...] = jnp.where(iota((8, rows_dev), 0) == 0, owner, rank)
    ids = dot((owner_hot * (local + 1.0)).astype(BF), hot(rank, LANES), ((1,), (1,))).astype(BF)
    slot = owner * capacity + rank
    group = max(1, 256 // capacity)
    arrivals[2].wait()
    departures = []
    for first in range(0, peers, group):
        packed = dot(hot(slot - first * capacity, group * capacity), rows_ref[...])
        for p in range(group):
            put_block(
                send_ref,
                (first + p) * block,
                packed[p * capacity : (p + 1) * capacity],
                jnp.broadcast_to(ids[first + p : first + p + 1], (META, LANES)),
            )
        part = pl.ds(first * block, group * block)
        departures.append(
            pltpu.make_async_copy(
                send_ref.at[part], send_hbm.at[part], out_sems.at[first // group]
            )
        )
        departures[-1].start()
    for copy in departures:
        copy.wait()


def pack_split_kernel(
    peers, capacity, cells_dev, distances, cell_hbm, place_hbm, rows_hbm, *refs
):
    send_hbms = refs[:peers]
    route_ref, cell_ref, place_ref, rows_ref, send_ref, in_sems, out_sems = refs[peers:]
    arrivals = fetch(
        (cell_hbm, place_hbm, rows_hbm), (cell_ref, place_ref, rows_ref), in_sems
    )
    rows_dev, width = rows_ref.shape
    block = (width // LANES) * capacity + META
    upper = prefix(rows_dev)
    me = lax.axis_index("wide")
    arrivals[0].wait()
    arrivals[1].wait()
    owner, local, rank, _ = find_route(cells_dev, peers, cell_ref, place_ref, upper)
    route_ref[...] = jnp.where(iota((8, rows_dev), 0) == 0, owner, rank)
    apart = owner ^ me
    order = jnp.zeros_like(owner)
    for i, r in enumerate(distances):
        order = jnp.where(apart == r, i, order)
    slot = order * capacity + rank
    ids = dot(
        (hot(order, peers, F32) * (local + 1.0)).astype(BF), hot(rank, LANES), ((1,), (1,))
    ).astype(BF)
    group = max(1, 256 // capacity)
    arrivals[2].wait()
    departures = []
    for first in range(0, peers, group):
        packed = dot(hot(slot - first * capacity, group * capacity), rows_ref[...])
        for p in range(group):
            i = first + p
            put_block(
                send_ref,
                i * block,
                packed[p * capacity : (p + 1) * capacity],
                jnp.broadcast_to(ids[i : i + 1], (META, LANES)),
            )
            departures.append(
                pltpu.make_async_copy(
                    send_ref.at[pl.ds(i * block, block)], send_hbms[i], out_sems.at[i]
                )
            )
            departures[-1].start()
    for copy in departures:
        copy.wait()


def seed_kernel(reseed_ref, rows_ref, seed_hbm, seed_ref, sems):
    rows_dev = rows_ref.shape[0]
    part = seed_ref.shape[0] // sems.shape[0]
    copies = []
    for i in range(sems.shape[0]):
        here = slice(i * part, (i + 1) * part)
        picked = hot(reseed_ref[:, here], rows_dev)
        seed_ref[here, :] = dot(picked, rows_ref[...], ((0,), (0,))).astype(BF)
        copies.append(
            pltpu.make_async_copy(seed_ref.at[here], seed_hbm.at[here], sems.at[i])
        )
        copies[-1].start()
    for copy in copies:
        copy.wait()


def score_kernel(blocks, capacity, far_of, known, coarse_ref, norm_ref, fine_ref, *refs):
    got_refs = refs[: len(blocks)]
    known_refs = refs[len(blocks) : len(blocks) + len(known)]
    error_ref, weight_ref, ids_ref, resid_hbm, resid_ref, sems = refs[len(blocks) + len(known) :]
    cells_dev, width = coarse_ref.shape
    fine_n = norm_ref.shape[1]
    chunks = width // LANES
    size = chunks * capacity + META
    group = max(1, 256 // capacity)
    tile = max(1, 512 // fine_n) * fine_n
    places = [(ref, b * size) for ref, count in zip(got_refs, blocks) for b in range(count)]
    error_ref[...] = jnp.zeros_like(error_ref)
    rows_of = list(range(len(places)))
    if far_of is not None:
        me = lax.axis_index("wide")
        rows_of = [me ^ r for r in far_of]
        half = error_ref.shape[0] // 2
        for ref, distances in zip(known_refs, known):
            for i in range(ref.shape[0]):
                row = (me & half) + i if distances is None else me ^ distances[i]
                error_ref[row] = ref[i]
    for p, (ref, base) in enumerate(places):
        ids_ref[:, p * capacity : (p + 1) * capacity] = (
            get_meta(ref, base, capacity, chunks)[0:1, :capacity].astype(jnp.int32) - 1
        )
    norms = split3(norm_ref[...])
    copies = []
    for first in range(0, len(places), group):
        some = places[first : first + group]
        span = len(some) * capacity
        here = slice(first * capacity, first * capacity + span)
        ids = ids_ref[:, here]
        member = hot(ids, cells_dev)
        own = dot(member, coarse_ref[...], ((0,), (0,)))
        square = jnp.zeros((span, LANES), F32)
        got = [get_block(ref, base, capacity, chunks) for ref, base in some]
        for j in range(chunks):
            lanes = slice(j * LANES, (j + 1) * LANES)
            part = (jnp.concatenate([g[j] for g in got], axis=0) - own[:, lanes]).astype(BF)
            resid_ref[here, lanes] = part
            wide = part.astype(F32)
            square += wide * wide
        resid = resid_ref[here, :]
        copies.append(
            pltpu.make_async_copy(resid_ref.at[here], resid_hbm.at[here], sems.at[first // group])
        )
        copies[-1].start()
        column = jnp.sum(square, axis=1, keepdims=True)
        diagonal = iota((span, span), 0) == iota((span, span), 1)
        square_row = jnp.sum(jnp.where(diagonal, column, 0.0), axis=0, keepdims=True)
        best = jnp.zeros((fine_n, span), F32)
        for start in range(0, cells_dev * fine_n, tile):
            scores = dot(fine_ref[start : start + tile, :], resid, ((1,), (1,)))
            for c in range(tile // fine_n):
                best = jnp.where(
                    ids == start // fine_n + c, scores[c * fine_n : (c + 1) * fine_n], best
                )
        norm = sum(dot(part, member, ((0,), (0,))) for part in norms)
        logit = (2.0 * best - norm) * (1.0 / TEMP)
        peak = jnp.max(logit, axis=0, keepdims=True)
        expo = jnp.exp(logit - peak)
        total = jnp.sum(expo, axis=0, keepdims=True)
        weight_ref[:, here] = (expo / total).astype(BF)
        error = square_row - TEMP * (peak + jnp.log(total))
        for p in range(len(some)):
            error_ref[rows_of[first + p], :, :capacity] = error[
                :, p * capacity : (p + 1) * capacity
            ]
    for copy in copies:
        copy.wait()


def update_kernel(sets, coarse_ref, *refs):
    ids_refs, weight_refs, resid_hbms = (refs[i * sets : (i + 1) * sets] for i in range(3))
    (
        seed_hbm, coarse_out_ref, fine_hbm, resid_ref, seed_ref, out_ref, spread_ref, share_ref,
        in_sems, seed_sems, out_sems,
    ) = refs[3 * sets :]
    cells_dev, width = coarse_ref.shape
    fine_n = weight_refs[0].shape[0]
    steps = out_sems.shape[0]
    cells = cells_dev // steps
    rows = cells * fine_n
    starts = [sum(r.shape[0] for r in resid_hbms[:i]) for i in range(sets)]
    arrivals = fetch(
        resid_hbms,
        [resid_ref.at[pl.ds(s, r.shape[0])] for s, r in zip(starts, resid_hbms)],
        in_sems,
    )
    half = seed_ref.shape[0] // 2
    parts = [pl.ds(0, half), pl.ds(half, half)]
    seeds = fetch([seed_hbm.at[p] for p in parts], [seed_ref.at[p] for p in parts], seed_sems)
    ids = jnp.concatenate([ref[...] for ref in ids_refs], axis=1)
    weight = jnp.concatenate([ref[...] for ref in weight_refs], axis=1).astype(F32)
    centre = coarse_ref[...].astype(F32)

    def spread(step):
        for c in range(cells):
            part = jnp.where(ids == step * cells + c, weight, 0.0)
            spread_ref[step % 2, c * fine_n : (c + 1) * fine_n, :] = part.astype(BF)
            first = step * rows + c * fine_n
            share_ref[first : first + fine_n, :] = jnp.broadcast_to(
                1.0 / (jnp.sum(part, axis=1, keepdims=True) + 1.0), (fine_n, LANES)
            )

    def finish(step):
        for c in range(cells):
            here = slice(step * rows + c * fine_n, step * rows + (c + 1) * fine_n)
            own = centre[step * cells + c : step * cells + c + 1]
            share = share_ref[here, :]
            for j in range(0, width, LANES):
                lanes = slice(j, j + LANES)
                seed = seed_ref[here, lanes].astype(F32) - own[:, lanes]
                out_ref[here, lanes] = (out_ref[here, lanes] + seed) * share
        part = pl.ds(step * rows, rows)
        copy = pltpu.make_async_copy(out_ref.at[part], fine_hbm.at[part], out_sems.at[step])
        copy.start()
        return copy

    spread(0)
    for copy in arrivals:
        copy.wait()
    departures = []
    for step in range(steps + 1):
        if step == 1:
            seeds[0].wait()
        if step == steps // 2 + 1:
            seeds[1].wait()
        if step < steps:
            out_ref[step * rows : (step + 1) * rows, :] = dot(spread_ref[step % 2], resid_ref[...])
        if step + 1 < steps:
            spread(step + 1)
        if step > 0:
            departures.append(finish(step - 1))
    member = hot(ids, cells_dev, F32)
    count = jnp.sum(member, axis=1, keepdims=True)
    coarse_out_ref[...] = centre + dot(member.astype(BF), resid_ref[...]) / (count + 1.0)
    for copy in departures:
        copy.wait()


def collect_kernel(peers, route_ref, error_ref, out_ref):
    owner_hot = hot(route_ref[0:1, :], peers, F32)
    rank_hot = hot(route_ref[1:2, :], LANES)
    error = error_ref[...].reshape(peers, LANES)
    picked = sum(dot(part, rank_hot) for part in split3(error))
    out_ref[...] = jnp.sum(picked * owner_hot, axis=0, keepdims=True)


def far(x):
    return pltpu.with_memory_space_constraint(x, pltpu.HBM)


def whole(shape):
    return pl.BlockSpec(shape, lambda *_: (0,) * len(shape))


HBM = pl.BlockSpec(memory_space=pltpu.HBM)
VMEM = pl.BlockSpec(memory_space=pltpu.VMEM)


def call(kernel, grid, in_specs, out_specs, out_shape, scratch=(), flops=0, moved=0):
    return pl.pallas_call(
        kernel,
        grid=grid,
        in_specs=in_specs,
        out_specs=out_specs,
        out_shape=out_shape,
        scratch_shapes=scratch,
        compiler_params=pltpu.CompilerParams(vmem_limit_bytes=VMEM_LIMIT),
        cost_estimate=pl.CostEstimate(flops=flops, bytes_accessed=moved, transcendentals=0),
    )


def shape_of(shape, dtype):
    return jax.ShapeDtypeStruct(shape, dtype)


def score(got, blocks, capacity, coarse, norm, fine, far_of=None, known=(), errors=(), peers=0):
    width = coarse.shape[1]
    fine_n = norm.shape[1]
    count = sum(blocks)
    slots = count * capacity
    return call(
        functools.partial(score_kernel, blocks, capacity, far_of, known),
        (),
        [VMEM] * (3 + len(got) + len(errors)),
        [VMEM, VMEM, VMEM, HBM],
        [
            shape_of((peers or count, 1, LANES), F32),
            shape_of((fine_n, slots), BF),
            shape_of((1, slots), jnp.int32),
            pltpu.HBM((slots, width), BF),
        ],
        scratch=[
            pltpu.VMEM((slots, width), BF),
            pltpu.SemaphoreType.DMA((count,)),
        ],
        flops=2 * slots * fine.shape[0] * width,
        moved=2 * (2 * slots + fine.shape[0]) * width,
    )(coarse, norm, fine, *got, *errors)


def update(scored, coarse, seed, cells_dev, fine_n):
    width = coarse.shape[1]
    fine_all = cells_dev * fine_n
    sets = len(scored)
    _, weights, ids, resids = zip(*scored)
    slots = sum(r.shape[0] for r in resids)
    steps = max(2, cells_dev // 4)
    coarse_new, fine_new = call(
        functools.partial(update_kernel, sets),
        (),
        [VMEM] * (1 + 2 * sets) + [HBM] * (sets + 1),
        [VMEM, HBM],
        [shape_of((cells_dev, width), F32), pltpu.HBM((fine_all, width), F32)],
        scratch=[
            pltpu.VMEM((slots, width), BF),
            pltpu.VMEM((fine_all, width), BF),
            pltpu.VMEM((fine_all, width), F32),
            pltpu.VMEM((2, fine_all // steps, slots), BF),
            pltpu.VMEM((fine_all, LANES), F32),
            pltpu.SemaphoreType.DMA((sets,)),
            pltpu.SemaphoreType.DMA((2,)),
            pltpu.SemaphoreType.DMA((steps,)),
        ],
        flops=2 * slots * fine_all * width,
        moved=2 * slots * width + 6 * fine_all * width,
    )(coarse, *ids, *weights, *[far(r) for r in resids], far(seed))
    return coarse_new, fine_new.reshape(cells_dev, fine_n, width)


def shards(rows, cell, cell_place, coarse, fine, reseed):
    peers = lax.axis_size("wide")
    rows_dev, width = rows.shape
    cells_dev, fine_n, _ = fine.shape
    cells = cell_place.shape[0]
    capacity = max(16, 2 * rows_dev // peers)
    slots = peers * capacity
    block = (width // LANES) * capacity + META
    fine_all = cells_dev * fine_n

    fine_wide = fine.astype(F32)
    norm = jnp.sum(fine_wide * fine_wide, axis=-1)
    fine_flat = fine.reshape(fine_all, width)
    seed = call(
        seed_kernel,
        (),
        [VMEM, VMEM],
        HBM,
        pltpu.HBM((fine_all, width), BF),
        scratch=[pltpu.VMEM((fine_all, width), BF), pltpu.SemaphoreType.DMA((4,))],
        flops=2 * fine_all * rows_dev * width,
        moved=2 * (fine_all + rows_dev) * width,
    )(reseed.reshape(1, fine_all), rows)
    cell = far(cell.reshape(1, rows_dev))
    cell_place = far(cell_place.reshape(1, cells))
    if capacity == 64 and peers == 16:
        distances = DISTANCES
        *sends, route = call(
            functools.partial(pack_split_kernel, peers, capacity, cells_dev, distances),
            (),
            [HBM] * 3,
            [HBM] * peers + [VMEM],
            [pltpu.HBM((block, LANES), BF)] * peers + [shape_of((8, rows_dev), jnp.int32)],
            scratch=[
                pltpu.VMEM((1, rows_dev), jnp.int32),
                pltpu.VMEM((1, cells), jnp.int32),
                pltpu.VMEM((rows_dev, width), BF),
                pltpu.VMEM((peers * block, LANES), BF),
                pltpu.SemaphoreType.DMA((3,)),
                pltpu.SemaphoreType.DMA((peers,)),
            ],
            flops=2 * slots * rows_dev * width,
            moved=2 * (slots + 2 * rows_dev) * width,
        )(cell, cell_place, far(rows))
        got = []
        for i, r in enumerate(distances):
            block_out = sends[i]
            if i >= WINDOW:
                block_out, got[i - WINDOW] = lax.optimization_barrier((block_out, got[i - WINDOW]))
            if r:
                block_out = lax.ppermute(block_out, "wide", [(p, p ^ r) for p in range(peers)])
            got.append(block_out)
        tables = (coarse, norm, fine_flat)
        scored = []
        for size in SIZES:
            first = sum(SIZES[: len(scored)])
            some = got[first : first + size]
            if first + size < peers:
                scored.append(score(some, [1] * size, capacity, *tables))
            else:
                ends = [sum(SIZES[: i + 1]) for i in range(len(scored))]
                known = tuple(distances[e - n : e] for e, n in zip(ends, SIZES))
                errors = [x[0] for x in scored]
                scored.append(
                    score(
                        some, [1] * size, capacity, *tables, distances[first:], known, errors, peers
                    )
                )
    else:
        send, route = call(
            functools.partial(pack_kernel, peers, capacity, cells_dev),
            (),
            [HBM] * 3,
            [HBM, VMEM],
            [pltpu.HBM((peers * block, LANES), BF), shape_of((8, rows_dev), jnp.int32)],
            scratch=[
                pltpu.VMEM((1, rows_dev), jnp.int32),
                pltpu.VMEM((1, cells), jnp.int32),
                pltpu.VMEM((rows_dev, width), BF),
                pltpu.VMEM((peers * block, LANES), BF),
                pltpu.SemaphoreType.DMA((3,)),
                pltpu.SemaphoreType.DMA((peers,)),
            ],
            flops=2 * slots * rows_dev * width,
            moved=2 * (slots + rows_dev) * width,
        )(cell, cell_place, far(rows))
        got = lax.all_to_all(
            send.reshape(peers, block, LANES), "wide", split_axis=0, concat_axis=0, tiled=False
        ).reshape(peers * block, LANES)
        scored = [score([got], [peers], capacity, coarse, norm, fine_flat)]

    returned = lax.all_to_all(scored[-1][0], "wide", split_axis=0, concat_axis=0, tiled=False)
    coarse_new, fine_new = update(scored, coarse, seed, cells_dev, fine_n)
    row_error = call(
        functools.partial(collect_kernel, peers),
        (),
        [VMEM, VMEM],
        VMEM,
        shape_of((1, rows_dev), F32),
        moved=4 * (8 * rows_dev + peers * LANES),
    )(route, returned).reshape(rows_dev)
    return row_error, coarse_new, fine_new


def solution(mesh):
    in_specs = (
        P(("groups", "wide"), None),
        P(("groups", "wide")),
        P("groups"),
        P(("groups", "wide"), None),
        P(("groups", "wide"), None, None),
        P(("groups", "wide"), None),
    )
    out_specs = (
        P(("groups", "wide")),
        P(("groups", "wide"), None),
        P(("groups", "wide"), None, None),
    )
    return jax.shard_map(shards, mesh=mesh, in_specs=in_specs, out_specs=out_specs, check_vma=False)
```

```python
import functools

import jax
import jax.numpy as jnp
from jax import lax
from jax.experimental import pallas as pl
from jax.experimental.pallas import tpu as pltpu
from jax.sharding import PartitionSpec as P

TEMP = 16
LANES = 128
META = 16
DISTANCES = [10, 6, 14, 7, 8, 4, 12, 5, 11, 2, 15, 3, 9, 1, 13, 0]
WINDOW = 6
SIZES = (4, 4, 6, 2)
VMEM_LIMIT = 24 * 1024 * 1024
BF = jnp.bfloat16
F32 = jnp.float32


def iota(shape, dim):
    return lax.broadcasted_iota(jnp.int32, shape, dim)


def hot(index, size, dtype=BF):
    return (iota((size, index.shape[1]), 0) == index).astype(F32).astype(dtype)


def dot(a, b, dims=((1,), (0,))):
    return lax.dot_general(a, b, (dims, ((), ())), preferred_element_type=F32)


def split3(x):
    high = x.astype(BF)
    rest = x - high.astype(F32)
    mid = rest.astype(BF)
    return high, mid, (rest - mid.astype(F32)).astype(BF)


def put_block(ref, base, rows, meta):
    count, width = rows.shape
    chunks = width // LANES
    whole_rows = count // 16 * 16
    for j in range(chunks):
        ref[base + j * whole_rows : base + (j + 1) * whole_rows, :] = rows[
            :whole_rows, j * LANES : (j + 1) * LANES
        ].astype(BF)
    base += chunks * whole_rows
    if count > whole_rows:
        for j in range(0, chunks, 2):
            pair = [
                rows[whole_rows:, i * LANES : (i + 1) * LANES] for i in (j, j + 1)
            ]
            ref[base : base + 16, :] = jnp.concatenate(pair, axis=0).astype(BF)
            base += 16
    ref[base : base + META, :] = meta


def get_block(ref, base, count, chunks):
    whole_rows = count // 16 * 16
    parts = [
        ref[base + j * whole_rows : base + (j + 1) * whole_rows, :].astype(F32)
        for j in range(chunks)
    ]
    if count > whole_rows:
        base += chunks * whole_rows
        for j in range(0, chunks, 2):
            pair = ref[base + j * 8 : base + j * 8 + 16, :].astype(F32)
            parts[j] = jnp.concatenate([parts[j], pair[:8]], axis=0)
            parts[j + 1] = jnp.concatenate([parts[j + 1], pair[8:]], axis=0)
    return parts


def get_meta(ref, base, count, chunks):
    first = base + chunks * count
    return ref[first : first + META, :].astype(F32)


def find_route(cells_dev, peers, cell_ref, place_ref, upper):
    rows_dev = cell_ref.shape[1]
    cells = place_ref.shape[1]
    cell = cell_ref[...]
    place = place_ref[...]
    table_row = iota((16, cells), 0)
    table = jnp.where(
        table_row == 0, place // cells_dev, jnp.where(table_row == 1, place % cells_dev, 0)
    ).astype(F32).astype(BF)
    found = jnp.zeros((16, rows_dev), F32)
    step = min(cells, 512)
    for first in range(0, cells, step):
        found += dot(table[:, first : first + step], hot(cell - first, step))
    owner = found[0:1].astype(jnp.int32)
    owner_hot = hot(owner, peers, F32)
    running = dot(owner_hot.astype(BF), upper)
    rank = (jnp.sum(running * owner_hot, axis=0, keepdims=True) - 1.0).astype(jnp.int32)
    return owner, found[1:2], rank, owner_hot


def prefix(rows_dev):
    return (iota((rows_dev, rows_dev), 0) <= iota((rows_dev, rows_dev), 1)).astype(F32).astype(BF)


def fetch(sources, targets, sems):
    copies = [
        pltpu.make_async_copy(source, target, sems.at[i])
        for i, (source, target) in enumerate(zip(sources, targets, strict=True))
    ]
    for copy in copies:
        copy.start()
    return copies


def pack_kernel(
    peers, capacity, cells_dev, cell_hbm, place_hbm, rows_hbm,
    send_hbm, route_ref, cell_ref, place_ref, rows_ref, send_ref, in_sems, out_sems,
):
    arrivals = fetch(
        (cell_hbm, place_hbm, rows_hbm), (cell_ref, place_ref, rows_ref), in_sems
    )
    rows_dev, width = rows_ref.shape
    block = (width // LANES) * capacity + META
    upper = prefix(rows_dev)
    arrivals[0].wait()
    arrivals[1].wait()
    owner, local, rank, owner_hot = find_route(cells_dev, peers, cell_ref, place_ref, upper)
    route_ref[...] = jnp.where(iota((8, rows_dev), 0) == 0, owner, rank)
    ids = dot((owner_hot * (local + 1.0)).astype(BF), hot(rank, LANES), ((1,), (1,))).astype(BF)
    slot = owner * capacity + rank
    group = max(1, 256 // capacity)
    arrivals[2].wait()
    departures = []
    for first in range(0, peers, group):
        packed = dot(hot(slot - first * capacity, group * capacity), rows_ref[...])
        for p in range(group):
            put_block(
                send_ref,
                (first + p) * block,
                packed[p * capacity : (p + 1) * capacity],
                jnp.broadcast_to(ids[first + p : first + p + 1], (META, LANES)),
            )
        part = pl.ds(first * block, group * block)
        departures.append(
            pltpu.make_async_copy(
                send_ref.at[part], send_hbm.at[part], out_sems.at[first // group]
            )
        )
        departures[-1].start()
    for copy in departures:
        copy.wait()


def pack_split_kernel(
    peers, capacity, cells_dev, distances, cell_hbm, place_hbm, rows_hbm, *refs
):
    send_hbms = refs[:peers]
    route_ref, cell_ref, place_ref, rows_ref, send_ref, in_sems, out_sems = refs[peers:]
    arrivals = fetch(
        (cell_hbm, place_hbm, rows_hbm), (cell_ref, place_ref, rows_ref), in_sems
    )
    rows_dev, width = rows_ref.shape
    block = (width // LANES) * capacity + META
    upper = prefix(rows_dev)
    me = lax.axis_index("wide")
    arrivals[0].wait()
    arrivals[1].wait()
    owner, local, rank, _ = find_route(cells_dev, peers, cell_ref, place_ref, upper)
    route_ref[...] = jnp.where(iota((8, rows_dev), 0) == 0, owner, rank)
    apart = owner ^ me
    order = jnp.zeros_like(owner)
    for i, r in enumerate(distances):
        order = jnp.where(apart == r, i, order)
    slot = order * capacity + rank
    ids = dot(
        (hot(order, peers, F32) * (local + 1.0)).astype(BF), hot(rank, LANES), ((1,), (1,))
    ).astype(BF)
    group = max(1, 256 // capacity)
    arrivals[2].wait()
    departures = []
    for first in range(0, peers, group):
        packed = dot(hot(slot - first * capacity, group * capacity), rows_ref[...])
        for p in range(group):
            i = first + p
            put_block(
                send_ref,
                i * block,
                packed[p * capacity : (p + 1) * capacity],
                jnp.broadcast_to(ids[i : i + 1], (META, LANES)),
            )
            departures.append(
                pltpu.make_async_copy(
                    send_ref.at[pl.ds(i * block, block)], send_hbms[i], out_sems.at[i]
                )
            )
            departures[-1].start()
    for copy in departures:
        copy.wait()


def seed_kernel(reseed_ref, rows_ref, seed_hbm, seed_ref, sems):
    rows_dev = rows_ref.shape[0]
    part = seed_ref.shape[0] // sems.shape[0]
    copies = []
    for i in range(sems.shape[0]):
        here = slice(i * part, (i + 1) * part)
        picked = hot(reseed_ref[:, here], rows_dev)
        seed_ref[here, :] = dot(picked, rows_ref[...], ((0,), (0,))).astype(BF)
        copies.append(
            pltpu.make_async_copy(seed_ref.at[here], seed_hbm.at[here], sems.at[i])
        )
        copies[-1].start()
    for copy in copies:
        copy.wait()


def score_kernel(blocks, capacity, far_of, known, coarse_ref, norm_ref, fine_ref, *refs):
    got_refs = refs[: len(blocks)]
    known_refs = refs[len(blocks) : len(blocks) + len(known)]
    error_ref, weight_ref, ids_ref, resid_hbm, resid_ref, sems = refs[len(blocks) + len(known) :]
    cells_dev, width = coarse_ref.shape
    fine_n = norm_ref.shape[1]
    chunks = width // LANES
    size = chunks * capacity + META
    group = max(1, 256 // capacity)
    tile = max(1, 512 // fine_n) * fine_n
    places = [(ref, b * size) for ref, count in zip(got_refs, blocks) for b in range(count)]
    error_ref[...] = jnp.zeros_like(error_ref)
    rows_of = list(range(len(places)))
    if far_of is not None:
        me = lax.axis_index("wide")
        rows_of = [me ^ r for r in far_of]
        half = error_ref.shape[0] // 2
        for ref, distances in zip(known_refs, known):
            for i in range(ref.shape[0]):
                row = (me & half) + i if distances is None else me ^ distances[i]
                error_ref[row] = ref[i]
    for p, (ref, base) in enumerate(places):
        ids_ref[:, p * capacity : (p + 1) * capacity] = (
            get_meta(ref, base, capacity, chunks)[0:1, :capacity].astype(jnp.int32) - 1
        )
    norms = split3(norm_ref[...])
    copies = []
    for first in range(0, len(places), group):
        some = places[first : first + group]
        span = len(some) * capacity
        here = slice(first * capacity, first * capacity + span)
        ids = ids_ref[:, here]
        member = hot(ids, cells_dev)
        own = dot(member, coarse_ref[...], ((0,), (0,)))
        square = jnp.zeros((span, LANES), F32)
        got = [get_block(ref, base, capacity, chunks) for ref, base in some]
        for j in range(chunks):
            lanes = slice(j * LANES, (j + 1) * LANES)
            part = (jnp.concatenate([g[j] for g in got], axis=0) - own[:, lanes]).astype(BF)
            resid_ref[here, lanes] = part
            wide = part.astype(F32)
            square += wide * wide
        resid = resid_ref[here, :]
        copies.append(
            pltpu.make_async_copy(resid_ref.at[here], resid_hbm.at[here], sems.at[first // group])
        )
        copies[-1].start()
        column = jnp.sum(square, axis=1, keepdims=True)
        diagonal = iota((span, span), 0) == iota((span, span), 1)
        square_row = jnp.sum(jnp.where(diagonal, column, 0.0), axis=0, keepdims=True)
        best = jnp.zeros((fine_n, span), F32)
        for start in range(0, cells_dev * fine_n, tile):
            scores = dot(fine_ref[start : start + tile, :], resid, ((1,), (1,)))
            for c in range(tile // fine_n):
                best = jnp.where(
                    ids == start // fine_n + c, scores[c * fine_n : (c + 1) * fine_n], best
                )
        norm = sum(dot(part, member, ((0,), (0,))) for part in norms)
        logit = (2.0 * best - norm) * (1.0 / TEMP)
        peak = jnp.max(logit, axis=0, keepdims=True)
        expo = jnp.exp(logit - peak)
        total = jnp.sum(expo, axis=0, keepdims=True)
        weight_ref[:, here] = (expo / total).astype(BF)
        error = square_row - TEMP * (peak + jnp.log(total))
        for p in range(len(some)):
            error_ref[rows_of[first + p], :, :capacity] = error[
                :, p * capacity : (p + 1) * capacity
            ]
    for copy in copies:
        copy.wait()


def update_kernel(sets, coarse_ref, *refs):
    ids_refs, weight_refs, resid_hbms = (refs[i * sets : (i + 1) * sets] for i in range(3))
    (
        seed_hbm, coarse_out_ref, fine_hbm, resid_ref, seed_ref, out_ref, spread_ref, share_ref,
        in_sems, seed_sems, out_sems,
    ) = refs[3 * sets :]
    cells_dev, width = coarse_ref.shape
    fine_n = weight_refs[0].shape[0]
    steps = out_sems.shape[0]
    cells = cells_dev // steps
    rows = cells * fine_n
    starts = [sum(r.shape[0] for r in resid_hbms[:i]) for i in range(sets)]
    arrivals = fetch(
        resid_hbms,
        [resid_ref.at[pl.ds(s, r.shape[0])] for s, r in zip(starts, resid_hbms)],
        in_sems,
    )
    half = seed_ref.shape[0] // 2
    parts = [pl.ds(0, half), pl.ds(half, half)]
    seeds = fetch([seed_hbm.at[p] for p in parts], [seed_ref.at[p] for p in parts], seed_sems)
    ids = jnp.concatenate([ref[...] for ref in ids_refs], axis=1)
    weight = jnp.concatenate([ref[...] for ref in weight_refs], axis=1).astype(F32)
    centre = coarse_ref[...].astype(F32)

    def spread(step):
        for c in range(cells):
            part = jnp.where(ids == step * cells + c, weight, 0.0)
            spread_ref[step % 2, c * fine_n : (c + 1) * fine_n, :] = part.astype(BF)
            first = step * rows + c * fine_n
            share_ref[first : first + fine_n, :] = jnp.broadcast_to(
                1.0 / (jnp.sum(part, axis=1, keepdims=True) + 1.0), (fine_n, LANES)
            )

    def finish(step):
        for c in range(cells):
            here = slice(step * rows + c * fine_n, step * rows + (c + 1) * fine_n)
            own = centre[step * cells + c : step * cells + c + 1]
            share = share_ref[here, :]
            for j in range(0, width, LANES):
                lanes = slice(j, j + LANES)
                seed = seed_ref[here, lanes].astype(F32) - own[:, lanes]
                out_ref[here, lanes] = (out_ref[here, lanes] + seed) * share
        part = pl.ds(step * rows, rows)
        copy = pltpu.make_async_copy(out_ref.at[part], fine_hbm.at[part], out_sems.at[step])
        copy.start()
        return copy

    spread(0)
    for copy in arrivals:
        copy.wait()
    departures = []
    for step in range(steps + 1):
        if step == 1:
            seeds[0].wait()
        if step == steps // 2 + 1:
            seeds[1].wait()
        if step < steps:
            out_ref[step * rows : (step + 1) * rows, :] = dot(spread_ref[step % 2], resid_ref[...])
        if step + 1 < steps:
            spread(step + 1)
        if step > 0:
            departures.append(finish(step - 1))
    member = hot(ids, cells_dev, F32)
    count = jnp.sum(member, axis=1, keepdims=True)
    coarse_out_ref[...] = centre + dot(member.astype(BF), resid_ref[...]) / (count + 1.0)
    for copy in departures:
        copy.wait()


def collect_kernel(peers, route_ref, error_ref, out_ref):
    owner_hot = hot(route_ref[0:1, :], peers, F32)
    rank_hot = hot(route_ref[1:2, :], LANES)
    error = error_ref[...].reshape(peers, LANES)
    picked = sum(dot(part, rank_hot) for part in split3(error))
    out_ref[...] = jnp.sum(picked * owner_hot, axis=0, keepdims=True)


def far(x):
    return pltpu.with_memory_space_constraint(x, pltpu.HBM)


def whole(shape):
    return pl.BlockSpec(shape, lambda *_: (0,) * len(shape))


HBM = pl.BlockSpec(memory_space=pltpu.HBM)
VMEM = pl.BlockSpec(memory_space=pltpu.VMEM)


def call(kernel, grid, in_specs, out_specs, out_shape, scratch=(), flops=0, moved=0):
    return pl.pallas_call(
        kernel,
        grid=grid,
        in_specs=in_specs,
        out_specs=out_specs,
        out_shape=out_shape,
        scratch_shapes=scratch,
        compiler_params=pltpu.CompilerParams(vmem_limit_bytes=VMEM_LIMIT),
        cost_estimate=pl.CostEstimate(flops=flops, bytes_accessed=moved, transcendentals=0),
    )


def shape_of(shape, dtype):
    return jax.ShapeDtypeStruct(shape, dtype)


def score(got, blocks, capacity, coarse, norm, fine, far_of=None, known=(), errors=(), peers=0):
    width = coarse.shape[1]
    fine_n = norm.shape[1]
    count = sum(blocks)
    slots = count * capacity
    return call(
        functools.partial(score_kernel, blocks, capacity, far_of, known),
        (),
        [VMEM] * (3 + len(got) + len(errors)),
        [VMEM, VMEM, VMEM, HBM],
        [
            shape_of((peers or count, 1, LANES), F32),
            shape_of((fine_n, slots), BF),
            shape_of((1, slots), jnp.int32),
            pltpu.HBM((slots, width), BF),
        ],
        scratch=[
            pltpu.VMEM((slots, width), BF),
            pltpu.SemaphoreType.DMA((count,)),
        ],
        flops=2 * slots * fine.shape[0] * width,
        moved=2 * (2 * slots + fine.shape[0]) * width,
    )(coarse, norm, fine, *got, *errors)


def update(scored, coarse, seed, cells_dev, fine_n):
    width = coarse.shape[1]
    fine_all = cells_dev * fine_n
    sets = len(scored)
    _, weights, ids, resids = zip(*scored)
    slots = sum(r.shape[0] for r in resids)
    steps = max(2, cells_dev // 4)
    coarse_new, fine_new = call(
        functools.partial(update_kernel, sets),
        (),
        [VMEM] * (1 + 2 * sets) + [HBM] * (sets + 1),
        [VMEM, HBM],
        [shape_of((cells_dev, width), F32), pltpu.HBM((fine_all, width), F32)],
        scratch=[
            pltpu.VMEM((slots, width), BF),
            pltpu.VMEM((fine_all, width), BF),
            pltpu.VMEM((fine_all, width), F32),
            pltpu.VMEM((2, fine_all // steps, slots), BF),
            pltpu.VMEM((fine_all, LANES), F32),
            pltpu.SemaphoreType.DMA((sets,)),
            pltpu.SemaphoreType.DMA((2,)),
            pltpu.SemaphoreType.DMA((steps,)),
        ],
        flops=2 * slots * fine_all * width,
        moved=2 * slots * width + 6 * fine_all * width,
    )(coarse, *ids, *weights, *[far(r) for r in resids], far(seed))
    return coarse_new, fine_new.reshape(cells_dev, fine_n, width)


def shards(rows, cell, cell_place, coarse, fine, reseed):
    peers = lax.axis_size("wide")
    rows_dev, width = rows.shape
    cells_dev, fine_n, _ = fine.shape
    cells = cell_place.shape[0]
    capacity = max(16, 2 * rows_dev // peers)
    slots = peers * capacity
    block = (width // LANES) * capacity + META
    fine_all = cells_dev * fine_n

    fine_wide = fine.astype(F32)
    norm = jnp.sum(fine_wide * fine_wide, axis=-1)
    fine_flat = fine.reshape(fine_all, width)
    seed = call(
        seed_kernel,
        (),
        [VMEM, VMEM],
        HBM,
        pltpu.HBM((fine_all, width), BF),
        scratch=[pltpu.VMEM((fine_all, width), BF), pltpu.SemaphoreType.DMA((4,))],
        flops=2 * fine_all * rows_dev * width,
        moved=2 * (fine_all + rows_dev) * width,
    )(reseed.reshape(1, fine_all), rows)
    cell = far(cell.reshape(1, rows_dev))
    cell_place = far(cell_place.reshape(1, cells))
    if capacity == 64 and peers == 16:
        distances = DISTANCES
        *sends, route = call(
            functools.partial(pack_split_kernel, peers, capacity, cells_dev, distances),
            (),
            [HBM] * 3,
            [HBM] * peers + [VMEM],
            [pltpu.HBM((block, LANES), BF)] * peers + [shape_of((8, rows_dev), jnp.int32)],
            scratch=[
                pltpu.VMEM((1, rows_dev), jnp.int32),
                pltpu.VMEM((1, cells), jnp.int32),
                pltpu.VMEM((rows_dev, width), BF),
                pltpu.VMEM((peers * block, LANES), BF),
                pltpu.SemaphoreType.DMA((3,)),
                pltpu.SemaphoreType.DMA((peers,)),
            ],
            flops=2 * slots * rows_dev * width,
            moved=2 * (slots + 2 * rows_dev) * width,
        )(cell, cell_place, far(rows))
        got = []
        for i, r in enumerate(distances):
            block_out = sends[i]
            if i >= WINDOW:
                block_out, got[i - WINDOW] = lax.optimization_barrier((block_out, got[i - WINDOW]))
            if r:
                block_out = lax.ppermute(block_out, "wide", [(p, p ^ r) for p in range(peers)])
            got.append(block_out)
        tables = (coarse, norm, fine_flat)
        scored = []
        for size in SIZES:
            first = sum(SIZES[: len(scored)])
            some = got[first : first + size]
            if first + size < peers:
                scored.append(score(some, [1] * size, capacity, *tables))
            else:
                ends = [sum(SIZES[: i + 1]) for i in range(len(scored))]
                known = tuple(distances[e - n : e] for e, n in zip(ends, SIZES))
                errors = [x[0] for x in scored]
                scored.append(
                    score(
                        some, [1] * size, capacity, *tables, distances[first:], known, errors, peers
                    )
                )
    else:
        send, route = call(
            functools.partial(pack_kernel, peers, capacity, cells_dev),
            (),
            [HBM] * 3,
            [HBM, VMEM],
            [pltpu.HBM((peers * block, LANES), BF), shape_of((8, rows_dev), jnp.int32)],
            scratch=[
                pltpu.VMEM((1, rows_dev), jnp.int32),
                pltpu.VMEM((1, cells), jnp.int32),
                pltpu.VMEM((rows_dev, width), BF),
                pltpu.VMEM((peers * block, LANES), BF),
                pltpu.SemaphoreType.DMA((3,)),
                pltpu.SemaphoreType.DMA((peers,)),
            ],
            flops=2 * slots * rows_dev * width,
            moved=2 * (slots + rows_dev) * width,
        )(cell, cell_place, far(rows))
        got = lax.all_to_all(
            send.reshape(peers, block, LANES), "wide", split_axis=0, concat_axis=0, tiled=False
        ).reshape(peers * block, LANES)
        scored = [score([got], [peers], capacity, coarse, norm, fine_flat)]

    returned = lax.all_to_all(scored[-1][0], "wide", split_axis=0, concat_axis=0, tiled=False)
    coarse_new, fine_new = update(scored, coarse, seed, cells_dev, fine_n)
    row_error = call(
        functools.partial(collect_kernel, peers),
        (),
        [VMEM, VMEM],
        VMEM,
        shape_of((1, rows_dev), F32),
        moved=4 * (8 * rows_dev + peers * LANES),
    )(route, returned).reshape(rows_dev)
    return row_error, coarse_new, fine_new


def solution(mesh):
    in_specs = (
        P(("groups", "wide"), None),
        P(("groups", "wide")),
        P("groups"),
        P(("groups", "wide"), None),
        P(("groups", "wide"), None, None),
        P(("groups", "wide"), None),
    )
    out_specs = (
        P(("groups", "wide")),
        P(("groups", "wide"), None),
        P(("groups", "wide"), None, None),
    )
    return jax.shard_map(shards, mesh=mesh, in_specs=in_specs, out_specs=out_specs, check_vma=False)
```
